32 devices in a mesh: batch: 8 (over z, x), mp: 4 (over y, core).
Axes of the slice: x: 2, y: 2, z: 4, core: 2. Of those that a mesh axis runs over, the one named last changes fastest.
Arguments:
- layer_tokens: bfloat16 [12288, 2048], P(('batch', 'mp')), may hold values from -6 to 6
- sequence_extents: int32 [8, 2], P('batch'), may hold values from 24 to 1416, as said below
- loss_sensitivity: bfloat16 [12288, 2048], P(('batch', 'mp')), may hold values from -6 to 6
- mixing_rms_gain: float32 [2048], replicated, may hold values from 0.5 to 1.5
- asker_dense_map: bfloat16 [2048, 2048], P(None, 'mp'), may hold values from -0.125 to 0.125
- lookup_dense_map: bfloat16 [2048, 512], P(None, 'mp'), may hold values from -0.125 to 0.125
- content_dense_map: bfloat16 [2048, 512], P(None, 'mp'), may hold values from -0.125 to 0.125
- shrink_map_asker: bfloat16 [2048, 8], replicated, may hold values from -0.125 to 0.125
- grow_map_asker: bfloat16 [8, 2048], P(None, 'mp'), may hold values from -0.3125 to 0.3125
- shrink_map_lookup: bfloat16 [2048, 8], replicated, may hold values from -0.125 to 0.125
- grow_map_lookup: bfloat16 [8, 512], P(None, 'mp'), may hold values from -0.3125 to 0.3125
- shrink_map_content: bfloat16 [2048, 8], replicated, may hold values from -0.125 to 0.125
- grow_map_content: bfloat16 [8, 512], P(None, 'mp'), may hold values from -0.3125 to 0.3125
- asker_feature_maps: float32 [32, 64, 64], P('mp'), may hold values from -0.75 to 0.75
- lookup_feature_maps: float32 [32, 64, 64], P('mp'), may hold values from -0.75 to 0.75
- local_portion_logit: float32 [32], P('mp'), may hold values from -2 to 2
- emitted_mixing_map: bfloat16 [2048, 2048], P('mp'), may hold values from -0.75 to 0.75
- emitted_shrink_map: bfloat16 [2048, 8], P('mp'), may hold values from -0.75 to 0.75
- emitted_grow_map: bfloat16 [8, 2048], replicated, may hold values from -0.3125 to 0.3125
- feedforward_rms_gain: float32 [2048], replicated, may hold values from 0.5 to 1.5
- gating_dense_map: bfloat16 [2048, 8192], P(None, 'mp'), may hold values from -0.125 to 0.125
- widen_dense_map: bfloat16 [2048, 8192], P(None, 'mp'), may hold values from -0.125 to 0.125
- shrink_dense_map: bfloat16 [8192, 2048], P('mp'), may hold values from -0.0625 to 0.0625
Outputs:
- output: bfloat16 [12288, 2048], P(('batch', 'mp'))
- input_grad: bfloat16 [12288, 2048], P(('batch', 'mp'))
- grad_norm_one: float32 [2048], replicated
- grad_w_query: float32 [2048, 2048], P(None, 'mp')
- grad_w_key: float32 [2048, 512], P(None, 'mp')
- grad_w_value: float32 [2048, 512], P(None, 'mp')
- grad_a_query: float32 [2048, 8], replicated
- asker_grow_derivative: float32 [8, 2048], P(None, 'mp')
- grad_a_key: float32 [2048, 8], replicated
- lookup_grow_derivative: float32 [8, 512], P(None, 'mp')
- grad_a_value: float32 [2048, 8], replicated
- content_grow_derivative: float32 [8, 512], P(None, 'mp')
- grad_query_maps: float32 [32, 64, 64], P('mp')
- grad_key_maps: float32 [32, 64, 64], P('mp')
- grad_window: float32 [32], P('mp')
- grad_w_out: float32 [2048, 2048], P('mp')
- grad_a_out: float32 [2048, 8], P('mp')
- emitted_grow_derivative: float32 [8, 2048], replicated
- grad_norm_two: float32 [2048], replicated
- grad_w_gate: float32 [2048, 8192], P(None, 'mp')
- grad_w_up: float32 [2048, 8192], P(None, 'mp')
- grad_w_down: float32 [8192, 2048], P('mp')
- teacher_mse: float32 [], replicated
The draws below stay inside these ranges and needn't reach their ends.
Inputs may be any that keep to these rules, and one draw needn't show every extreme that they name: `sequence_extents`: group g's 2 sequences fill its first rows in order; the rest of its 1536 rows, fewer than 384, are padding. In every group one sequence begins among the first 384 rows and ends among the last 384.
All inputs are finite; a program needn't handle non-finite values.
Results may differ from the reference program's by a relative error of at most 0.025.
Values may be sent and summed in bfloat16 or wider, within the bound.
No kernel may reach another device: no remote copies, remote signals or barrier semaphores. Data moves between devices by JAX's collectives and lax.ppermute only.
A program may use at most 576 MiB of HBM per device.

```python
import jax
import jax.numpy as jnp
from jax import lax

EMBED_WIDTH = 2048
ASKER_COUNT = 32
KV_HEADS = 8
CHANNEL_SIZE = 64
FF = 8192
MAP = 64
FACTOR_SIZE = 8
WINDOW = 64
QBLOCK = 512
SEQS = 2
GROUP_TOK = 1536
TOKENS = 12288
N_BATCH = 8
N_MP = 4


def draw_sequence_extents(key, part):
    block_rows = GROUP_TOK // N_MP
    least_len = max(1, block_rows // 16)
    subkeys = jax.random.split(key, 4)
    padding = jax.random.randint(subkeys[0], (N_BATCH,), block_rows // 4, block_rows // 2)
    shorter = jax.random.randint(subkeys[1], (N_BATCH,), least_len, block_rows // 2)
    first_bit = jax.random.randint(subkeys[2], (N_BATCH,), 0, 2)
    chosen = jax.random.randint(subkeys[3], (), 0, N_BATCH)
    picked = jnp.arange(N_BATCH) == chosen
    padding = jnp.where(picked, block_rows // 4, padding)
    shorter = jnp.where(picked, least_len, shorter)
    longer = GROUP_TOK - padding - shorter
    leading = jnp.where(first_bit == 0, longer, shorter)
    trailing = jnp.where(first_bit == 0, shorter, longer)
    return jnp.stack([leading, trailing], axis=1).astype(jnp.int32)


def block_levels(own_key, shape, cuts, smallest, high):
    level, own = 1.0, jax.random.fold_in(own_key, 6)
    for axis_at, parts in cuts:
        heights = jnp.exp(jax.random.uniform(jax.random.fold_in(own, axis_at), (parts,), jnp.float32, smallest / len(cuts), high / len(cuts)))
        level = level * jnp.repeat(heights, shape[axis_at] // parts).reshape([-1 if axis == axis_at else 1 for axis in range(len(shape))])
    return level


def centred(own_key, extent, scale, most, shards=(), kind=jnp.bfloat16):
    array = jax.random.normal(own_key, extent, jnp.float32) * scale
    if len(shards) > 0:
        array = block_levels(own_key, extent, shards, -0.22, 0.18) * array
    return jnp.clip(array, min=-most, max=most).astype(kind)


def setup_inputs(seed: int = 0) -> dict:
    arg_keys = jax.random.split(jax.random.key(seed), 24)
    layer_tokens = centred(arg_keys[0], (TOKENS, EMBED_WIDTH), 1.0, 6.0, ((0, 32),))
    sequence_extents = draw_sequence_extents(jax.random.fold_in(arg_keys[23], 71), 0)
    loss_sensitivity = centred(arg_keys[2], (TOKENS, EMBED_WIDTH), 1.0, 6.0, ((0, 32),))
    mixing_rms_gain = jnp.clip(1.0 + 0.1 * jax.random.normal(arg_keys[3], (EMBED_WIDTH,), jnp.float32), 0.5, 1.5)
    asker_dense_map = centred(arg_keys[4], (EMBED_WIDTH, ASKER_COUNT * CHANNEL_SIZE), EMBED_WIDTH ** -0.5, 0.125, ((1, 4),))
    lookup_dense_map = centred(arg_keys[5], (EMBED_WIDTH, KV_HEADS * CHANNEL_SIZE), EMBED_WIDTH ** -0.5, 0.125, ((1, 4),))
    content_dense_map = centred(arg_keys[6], (EMBED_WIDTH, KV_HEADS * CHANNEL_SIZE), EMBED_WIDTH ** -0.5, 0.125, ((1, 4),))
    shrink_map_asker = centred(arg_keys[7], (EMBED_WIDTH, FACTOR_SIZE), EMBED_WIDTH ** -0.5, 0.125)
    grow_map_asker = centred(arg_keys[8], (FACTOR_SIZE, ASKER_COUNT * CHANNEL_SIZE), 384 ** -0.5, 0.3125, ((1, 4),))
    shrink_map_lookup = centred(arg_keys[9], (EMBED_WIDTH, FACTOR_SIZE), EMBED_WIDTH ** -0.5, 0.125)
    grow_map_lookup = centred(arg_keys[10], (FACTOR_SIZE, KV_HEADS * CHANNEL_SIZE), 384 ** -0.5, 0.3125, ((1, 4),))
    shrink_map_content = centred(arg_keys[11], (EMBED_WIDTH, FACTOR_SIZE), EMBED_WIDTH ** -0.5, 0.125)
    grow_map_content = centred(arg_keys[12], (FACTOR_SIZE, KV_HEADS * CHANNEL_SIZE), 384 ** -0.5, 0.3125, ((1, 4),))
    asker_feature_maps = centred(arg_keys[13], (ASKER_COUNT, CHANNEL_SIZE, MAP), CHANNEL_SIZE ** -0.5, 0.75, ((0, 4),), jnp.float32)
    lookup_feature_maps = centred(arg_keys[14], (ASKER_COUNT, CHANNEL_SIZE, MAP), CHANNEL_SIZE ** -0.5, 0.75, ((0, 4),), jnp.float32)
    local_portion_logit = jnp.clip(jax.random.uniform(arg_keys[15], (ASKER_COUNT,), jnp.float32, -2.0, 2.0) * block_levels(arg_keys[15], (ASKER_COUNT,), ((0, 4),), -0.4, 0.0), -2.0, 2.0)
    emitted_mixing_map = centred(arg_keys[16], (ASKER_COUNT * CHANNEL_SIZE, EMBED_WIDTH), CHANNEL_SIZE ** -0.5, 0.75, ((0, 4),))
    emitted_shrink_map = centred(arg_keys[17], (ASKER_COUNT * CHANNEL_SIZE, FACTOR_SIZE), CHANNEL_SIZE ** -0.5, 0.75, ((0, 4),))
    emitted_grow_map = centred(arg_keys[18], (FACTOR_SIZE, EMBED_WIDTH), 384 ** -0.5, 0.3125)
    feedforward_rms_gain = jnp.clip(1.0 + 0.1 * jax.random.normal(arg_keys[19], (EMBED_WIDTH,), jnp.float32), 0.5, 1.5)
    gating_dense_map = centred(arg_keys[20], (EMBED_WIDTH, FF), EMBED_WIDTH ** -0.5, 0.125, ((1, 4),))
    widen_dense_map = centred(arg_keys[21], (EMBED_WIDTH, FF), EMBED_WIDTH ** -0.5, 0.125, ((1, 4),))
    shrink_dense_map = centred(arg_keys[22], (FF, EMBED_WIDTH), FF ** -0.5, 0.0625, ((0, 4),))
    return dict(layer_tokens=layer_tokens, sequence_extents=sequence_extents, loss_sensitivity=loss_sensitivity, mixing_rms_gain=mixing_rms_gain, asker_dense_map=asker_dense_map, lookup_dense_map=lookup_dense_map, content_dense_map=content_dense_map, shrink_map_asker=shrink_map_asker, grow_map_asker=grow_map_asker, shrink_map_lookup=shrink_map_lookup, grow_map_lookup=grow_map_lookup, shrink_map_content=shrink_map_content, grow_map_content=grow_map_content, asker_feature_maps=asker_feature_maps, lookup_feature_maps=lookup_feature_maps, local_portion_logit=local_portion_logit, emitted_mixing_map=emitted_mixing_map, emitted_shrink_map=emitted_shrink_map, emitted_grow_map=emitted_grow_map, feedforward_rms_gain=feedforward_rms_gain, gating_dense_map=gating_dense_map, widen_dense_map=widen_dense_map, shrink_dense_map=shrink_dense_map)


norm_eps = 1e-05
rope_base = 500000.0
factored_multiplier = 2.0
transfer_weight = 0.5
exactness_setting = lax.Precision.HIGHEST

@jax.custom_vjp
def low(v):
    return lax.optimization_barrier(v.astype(jnp.bfloat16)).astype(jnp.float32)

@jax.custom_vjp
def low_back(v):
    return v

def low_keep(v):
    return (low(v), None)

def low_pass(kept, grad):
    return (grad,)

def back_keep(v):
    return (v, None)

def back_low(kept, grad):
    return (low(grad),)
low.defvjp(low_keep, low_pass)
low_back.defvjp(back_keep, back_low)

def tensor_contract(left, right):
    return jnp.dot(left, right, precision=exactness_setting, preferred_element_type=jnp.float32)

def segments(lengths_row, group_rows):
    seg_ends = jnp.cumsum(lengths_row).astype(jnp.int32)
    places = jnp.arange(group_rows, dtype=jnp.int32)
    segment = lax.optimization_barrier(jnp.sum((places[:, None] >= seg_ends[None, :]).astype(jnp.int32), axis=1, dtype=jnp.int32))
    starts = jnp.concatenate([jnp.zeros((1,), jnp.int32), seg_ends])
    labels = jnp.arange(SEQS + 1, dtype=jnp.int32)
    picked = segment[:, None] == labels[None, :]
    position = places - lax.optimization_barrier(jnp.sum(jnp.where(picked, starts[None, :], 0), axis=1, dtype=jnp.int32))
    return (segment, position)

def rotate(values, position):
    half_head = CHANNEL_SIZE // 2
    frequency = rope_base ** (-2.0 * jnp.arange(half_head, dtype=jnp.float32) / CHANNEL_SIZE)
    angles = position.astype(jnp.float32)[:, None] * frequency[None, :]
    cosine = jnp.cos(angles)[:, None, :]
    sine_part = jnp.sin(angles)[:, None, :]
    front_half = values[..., :half_head]
    back_half = values[..., half_head:]
    return jnp.concatenate([front_half * cosine - back_half * sine_part, back_half * cosine + front_half * sine_part], axis=-1)

def feature(values, maps):
    projected_output = jnp.einsum('ghe,hem->ghm', values, maps, precision=exactness_setting)
    upper_exp = jnp.exp(projected_output)
    lower_exp = jnp.exp(-projected_output)
    return jnp.concatenate([upper_exp / lax.optimization_barrier(jnp.sum(upper_exp, axis=-1, keepdims=True)), lower_exp / lax.optimization_barrier(jnp.sum(lower_exp, axis=-1, keepdims=True))], axis=-1)

def with_previous(blocked, fill_value):
    before = jnp.concatenate([jnp.full_like(blocked[:1], fill_value), blocked[:-1]], axis=0)
    return jnp.concatenate([before, blocked], axis=1)

def attend(queries, key_rows, value_rows, asker_feature_maps, lookup_feature_maps, local_portion_logit, segment, position):
    group_rows = queries.shape[0]
    head_count = queries.shape[1]
    repeats = head_count // key_rows.shape[1]
    key_rows = jnp.repeat(key_rows, repeats, axis=1)
    value_rows = jnp.repeat(value_rows, repeats, axis=1)
    queries = rotate(queries, position)
    key_rows = rotate(key_rows, position)
    query_feat = feature(queries, asker_feature_maps)
    key_feat = feature(key_rows, lookup_feature_maps)
    score_scale = CHANNEL_SIZE ** (-0.5)
    blocks = group_rows // WINDOW
    feat_width = query_feat.shape[-1]
    query_blocks = queries.reshape(blocks, WINDOW, head_count, CHANNEL_SIZE)
    key_blocks = key_rows.reshape(blocks, WINDOW, head_count, CHANNEL_SIZE)
    value_blocks = value_rows.reshape(blocks, WINDOW, head_count, CHANNEL_SIZE)
    query_feat_blocks = query_feat.reshape(blocks, WINDOW, head_count, feat_width)
    key_feat_blocks = key_feat.reshape(blocks, WINDOW, head_count, feat_width)
    key_pairs = with_previous(key_blocks, 0.0)
    value_pairs = with_previous(value_blocks, 0.0)
    feat_pairs = with_previous(key_feat_blocks, 0.0)
    seg_blocks = segment.reshape(blocks, WINDOW)
    seg_pairs = with_previous(seg_blocks, -1)
    place_blocks = jnp.arange(group_rows, dtype=jnp.int32).reshape(blocks, WINDOW)
    place_pairs = jnp.concatenate([place_blocks - WINDOW, place_blocks], axis=1)
    distance = place_blocks[:, :, None] - place_pairs[:, None, :]
    same_seg = seg_blocks[:, :, None] == seg_pairs[:, None, :]
    near_mask = (same_seg & (distance >= 0) & (distance < WINDOW))[:, None]
    far_mask = (same_seg & (distance >= WINDOW))[:, None]
    scores = jnp.einsum('cihe,cjhe->chij', query_blocks, key_pairs, precision=exactness_setting) * score_scale
    kernel = jnp.einsum('cihf,cjhf->chij', query_feat_blocks, feat_pairs, precision=exactness_setting)
    window_share = jax.nn.sigmoid(local_portion_logit)
    keep_share = 1.0 - window_share
    weights = jnp.where(near_mask, window_share[None, :, None, None] * jnp.exp(scores), 0.0) + jnp.where(far_mask, keep_share[None, :, None, None] * kernel, 0.0)
    near_sum = jnp.einsum('chij,cjhe->cihe', weights, value_pairs, precision=exactness_setting)
    near_norm = jnp.transpose(lax.optimization_barrier(jnp.sum(weights, axis=3)), (0, 2, 1))
    member = (seg_blocks[:, :, None] == jnp.arange(SEQS + 1, dtype=jnp.int32)[None, None, :]).astype(jnp.float32)
    sorted_feat = member[:, :, :, None, None] * key_feat_blocks[:, :, None]
    states = jnp.einsum('cjshf,cjhe->cshfe', sorted_feat, value_blocks, precision=exactness_setting)
    state_norms = lax.optimization_barrier(jnp.sum(sorted_feat, axis=1))
    block_order = jnp.arange(blocks, dtype=jnp.int32)
    earlier = (block_order[:, None] >= block_order[None, :] + 2).astype(jnp.float32)
    prefix = jnp.einsum('xc,cshfe->xshfe', earlier, states, precision=exactness_setting)
    prefix_norms = jnp.einsum('xc,cshf->xshf', earlier, state_norms, precision=exactness_setting)
    far_all = jnp.einsum('cihf,cshfe->cishe', query_feat_blocks, prefix, precision=exactness_setting)
    far_sum = lax.optimization_barrier(jnp.sum(member[:, :, :, None, None] * far_all, axis=2))
    far_norm_all = jnp.einsum('cihf,cshf->cish', query_feat_blocks, prefix_norms, precision=exactness_setting)
    far_norm = lax.optimization_barrier(jnp.sum(member[:, :, :, None] * far_norm_all, axis=2))
    numerator = near_sum + keep_share[None, None, :, None] * far_sum
    denominator = near_norm + keep_share[None, None, :] * far_norm
    mixed = (numerator / denominator[..., None]).reshape(group_rows, head_count, CHANNEL_SIZE)
    places = jnp.arange(group_rows, dtype=jnp.int32)
    teacher_blocks = group_rows // QBLOCK

    def teacher_part(pieces):
        block_query, block_seg, block_place, block_mixed = pieces
        logits = jnp.einsum('ihe,jhe->hij', block_query, key_rows, precision=exactness_setting) * score_scale
        allowed = ((block_seg[:, None] == segment[None, :]) & (block_place[:, None] >= places[None, :]))[None]
        exponent = jnp.where(allowed, jnp.exp(logits), 0.0)
        teacher = jnp.einsum('hij,jhe->ihe', exponent, value_rows, precision=exactness_setting) / jnp.transpose(lax.optimization_barrier(jnp.sum(exponent, axis=2)))[:, :, None]
        missing = jnp.where((block_seg < SEQS)[:, None, None], block_mixed - teacher, 0.0)
        return jnp.sum(missing * missing)
    partials = lax.map(jax.checkpoint(teacher_part), (queries.reshape(teacher_blocks, QBLOCK, head_count, CHANNEL_SIZE), segment.reshape(teacher_blocks, QBLOCK), places.reshape(teacher_blocks, QBLOCK), mixed.reshape(teacher_blocks, QBLOCK, head_count, CHANNEL_SIZE)))
    return (mixed, jnp.sum(partials))

def rms_scale(values):
    return lax.rsqrt(lax.optimization_barrier(jnp.mean(values * values, axis=-1, keepdims=True)) + norm_eps)

def block_forward(model_parameters, residual_in, segment, position):
    mixing_rms_gain, asker_dense_map, lookup_dense_map, content_dense_map, shrink_map_asker, grow_map_asker, shrink_map_lookup, grow_map_lookup, shrink_map_content, grow_map_content, asker_feature_maps, lookup_feature_maps, local_portion_logit, emitted_mixing_map, emitted_shrink_map, emitted_grow_map, feedforward_rms_gain, gating_dense_map, widen_dense_map, shrink_dense_map = model_parameters
    normalized_input = low(residual_in * rms_scale(residual_in) * mixing_rms_gain)

    def project(weight_matrix, adapter_down_matrix, adapter_up_matrix):
        middle = low_back(low(tensor_contract(normalized_input, adapter_down_matrix)))
        return low_back(low(tensor_contract(normalized_input, weight_matrix) + factored_multiplier * tensor_contract(middle, adapter_up_matrix)))
    query_proj = project(asker_dense_map, shrink_map_asker, grow_map_asker)
    key_proj = project(lookup_dense_map, shrink_map_lookup, grow_map_lookup)
    value_proj = project(content_dense_map, shrink_map_content, grow_map_content)
    group_rows = residual_in.shape[0]
    group_ratio = ASKER_COUNT // KV_HEADS
    query_split = jnp.transpose(query_proj.reshape(group_rows, KV_HEADS, group_ratio, CHANNEL_SIZE), (1, 0, 2, 3))
    key_split = jnp.transpose(key_proj.reshape(group_rows, KV_HEADS, 1, CHANNEL_SIZE), (1, 0, 2, 3))
    value_split = jnp.transpose(value_proj.reshape(group_rows, KV_HEADS, 1, CHANNEL_SIZE), (1, 0, 2, 3))
    maps_query = asker_feature_maps.reshape(KV_HEADS, group_ratio, CHANNEL_SIZE, MAP)
    maps_key = lookup_feature_maps.reshape(KV_HEADS, group_ratio, CHANNEL_SIZE, MAP)
    window_split = local_portion_logit.reshape(KV_HEADS, group_ratio)

    def head_group(pieces):
        return attend(pieces[0], pieces[1], pieces[2], pieces[3], pieces[4], pieces[5], segment, position)
    mixed_split, teacher_split = lax.map(jax.checkpoint(head_group), (query_split, key_split, value_split, maps_query, maps_key, window_split))
    mixed = jnp.transpose(mixed_split, (1, 0, 2, 3)).reshape(group_rows, ASKER_COUNT * CHANNEL_SIZE)
    mixing_outcome = low(mixed)
    emitted_middle = low_back(low(tensor_contract(mixing_outcome, emitted_shrink_map)))
    factored_path = low_back(tensor_contract(mixing_outcome, emitted_mixing_map) + factored_multiplier * tensor_contract(emitted_middle, emitted_grow_map))
    hidden = residual_in + factored_path
    normed_two = low(hidden * rms_scale(hidden) * feedforward_rms_gain)
    gate_proj = low_back(tensor_contract(normed_two, gating_dense_map))
    up_proj = low_back(tensor_contract(normed_two, widen_dense_map))
    active = low(gate_proj * jax.nn.sigmoid(gate_proj) * up_proj)
    return (hidden + tensor_contract(active, shrink_dense_map), jnp.sum(teacher_split))

def reference(layer_tokens, sequence_extents, loss_sensitivity, mixing_rms_gain, asker_dense_map, lookup_dense_map, content_dense_map, shrink_map_asker, grow_map_asker, shrink_map_lookup, grow_map_lookup, shrink_map_content, grow_map_content, asker_feature_maps, lookup_feature_maps, local_portion_logit, emitted_mixing_map, emitted_shrink_map, emitted_grow_map, feedforward_rms_gain, gating_dense_map, widen_dense_map, shrink_dense_map):
    model_parameters = tuple((entry_tensor.astype(jnp.float32) for entry_tensor in (mixing_rms_gain, asker_dense_map, lookup_dense_map, content_dense_map, shrink_map_asker, grow_map_asker, shrink_map_lookup, grow_map_lookup, shrink_map_content, grow_map_content, asker_feature_maps, lookup_feature_maps, local_portion_logit, emitted_mixing_map, emitted_shrink_map, emitted_grow_map, feedforward_rms_gain, gating_dense_map, widen_dense_map, shrink_dense_map)))
    rows_in = layer_tokens.astype(jnp.float32).reshape(N_BATCH, GROUP_TOK, EMBED_WIDTH)
    cot_in = loss_sensitivity.astype(jnp.float32).reshape(N_BATCH, GROUP_TOK, EMBED_WIDTH)
    zeros_grad = jax.tree.map(jnp.zeros_like, model_parameters)

    def group_step(carried, group_in):
        grad_total, square_total = carried
        group_rows_in, group_cot, group_len = group_in
        segment, position = segments(group_len, GROUP_TOK)

        def forward(param_set, residual_in):
            return block_forward(param_set, residual_in, segment, position)
        (result, teacher_sq), pullback = jax.vjp(forward, model_parameters, group_rows_in)
        param_grads, input_grads = pullback((group_cot, jnp.float32(transfer_weight)))
        grad_total = jax.tree.map(jnp.add, grad_total, param_grads)
        return ((grad_total, square_total + teacher_sq), (result.astype(jnp.bfloat16), input_grads.astype(jnp.bfloat16)))
    (grad_total, square_total), (outputs, input_grads) = lax.scan(group_step, (zeros_grad, jnp.float32(0.0)), (rows_in, cot_in, sequence_extents))
    teacher_mse = square_total / (TOKENS * ASKER_COUNT * CHANNEL_SIZE)
    return (outputs.reshape(TOKENS, EMBED_WIDTH), input_grads.reshape(TOKENS, EMBED_WIDTH), grad_total[0], grad_total[1], grad_total[2], grad_total[3], grad_total[4], grad_total[5], grad_total[6], grad_total[7], grad_total[8], grad_total[9], grad_total[10], grad_total[11], grad_total[12], grad_total[13], grad_total[14], grad_total[15], grad_total[16], grad_total[17], grad_total[18], grad_total[19], teacher_mse)
```

```python
import functools
import math
import jax
import jax.numpy as jnp
from jax import lax
from jax.experimental import pallas as pl
from jax.experimental.pallas import tpu as pltpu
from jax.sharding import PartitionSpec as P

HD = 64
WINDOW = 64
CHUNK = 256
BACK = 128
LOG2E = math.log2(math.e)
LN2 = math.log(2.0)
BIG = 16384.0
F32 = jnp.float32
BF = jnp.bfloat16


def dot_nn(a, b):
    return lax.dot_general(a, b, (((1,), (0,)), ((), ())), preferred_element_type=F32)


def dot_nt(a, b):
    return lax.dot_general(a, b, (((1,), (1,)), ((), ())), preferred_element_type=F32)


def dot_tn(a, b):
    return lax.dot_general(a, b, (((0,), (0,)), ((), ())), preferred_element_type=F32)


def lanes(rows):
    return lax.broadcasted_iota(jnp.int32, (rows, 128), 1)


def swap(x):
    return pltpu.roll(x, 64, 1)


def spin(x):
    lane = lanes(x.shape[0])
    return jnp.where((lane & 63) < 32, pltpu.roll(x, 96, 1), pltpu.roll(x, 32, 1))


def twin(x, odd):
    low = lanes(x.shape[0]) < 64
    other = swap(x)
    return jnp.where(low != odd, x, other)


def half_ones():
    r = lax.broadcasted_iota(jnp.int32, (128, 128), 0)
    c = lax.broadcasted_iota(jnp.int32, (128, 128), 1)
    return ((r < 64) == (c < 64)).astype(BF)


def start_of(t, e0, e1):
    return jnp.where(t >= e1, e1, jnp.where(t >= e0, e0, 0))


def start_col(r0, rows, e0, e1):
    t = r0 + lax.broadcasted_iota(jnp.int32, (rows, 1), 0)
    return start_of(t, e0, e1)


def prep_keys(k_ref, v_ref, cos_ref, sin_ref, kaug, vaug, seg, e0, e1):
    T = k_ref.shape[0]
    for r0 in range(0, T, CHUNK):
        rows = pl.ds(r0, CHUNK)
        k = k_ref[rows, :].astype(F32)
        v = v_ref[rows, :].astype(F32)
        kr = k * cos_ref[rows, :] + spin(k) * sin_ref[rows, :]
        lane = lanes(CHUNK)
        low = lane < 64
        if seg:
            t = r0 + lax.broadcasted_iota(jnp.int32, (CHUNK, 1), 0)
            mine = (t >= e0).astype(jnp.int32) + (t >= e1).astype(jnp.int32) + 64
            tail = jnp.where((lane < 67) & (lane != mine), -BIG, 0.0)
        else:
            tail = 0.0
        for kv in range(2):
            x = twin(kr, kv == 1)
            hi = x.astype(BF)
            lo = x - hi.astype(F32)
            kaug[kv, rows, 0:128] = hi
            kaug[kv, rows, 128:256] = jnp.where(low, lo, tail).astype(BF)
            vaug[kv, rows, :] = jnp.where(low, v if kv == 0 else swap(v), 1.0).astype(BF)


def prep_query(qr, odd, seg, r0, e0, e1):
    x = twin(qr, odd)
    hi = x.astype(BF)
    lo = (x - hi.astype(F32)).astype(BF)
    lane = lanes(x.shape[0])
    low = lane < 64
    first = jnp.where(low, hi, lo)
    second = hi
    if seg:
        t = r0 + lax.broadcasted_iota(jnp.int32, (x.shape[0], 1), 0)
        mine = (t >= e0).astype(jnp.int32) + (t >= e1).astype(jnp.int32) + 64
        second = jnp.where(low, hi.astype(F32), jnp.where(lane == mine, 1.0, 0.0)).astype(BF)
    return first, second


def features(aug, maps, ones):
    p = jnp.exp2(dot_nn(aug, maps))
    return p / dot_nn(p.astype(BF), ones)


def fwd_kernel(e_ref, c_ref, q_ref, k_ref, v_ref, cos_ref, sin_ref, mq_ref, mk_ref,
               att_ref, nm_ref, kaug, vaug, qaug, phq, phk, *, rep):
    T = q_ref.shape[0]
    e0, e1 = e_ref[0], e_ref[1]
    p = pl.program_id(0)

    @pl.when(p == 0)
    def _():
        prep_keys(k_ref, v_ref, cos_ref, sin_ref, kaug, vaug, False, e0, e1)

    kv = (2 * p) // rep
    ones = half_ones()
    low = lanes(CHUNK) < 64
    for r0 in range(0, T, CHUNK):
        rows = pl.ds(r0, CHUNK)
        q = q_ref[rows, :].astype(F32) * (LOG2E / 8.0)
        qr = q * cos_ref[rows, :] + spin(q) * sin_ref[rows, :]
        for hh in range(2):
            first, second = prep_query(qr, hh == 1, False, r0, e0, e1)
            qaug[hh, rows, 0:128] = first
            qaug[hh, rows, 128:256] = second
            c = c_ref[2 * p + hh]
            phq[hh, rows, :] = (features(qaug[hh, rows, :], mq_ref[hh], ones) * c).astype(BF)
            phk[hh, rows, :] = features(kaug[kv, rows, :], mk_ref[hh], ones).astype(BF)
    for hh in range(2):
        state = None
        for r0 in range(0, T, CHUNK):
            rows = pl.ds(r0, CHUNK)
            j0 = max(r0 - BACK, 0)
            J = r0 + CHUNK - j0
            win = pl.ds(j0, J)
            ee = jnp.exp2(dot_nt(qaug[hh, rows, :], kaug[kv, win, :]))
            kap = dot_nt(phq[hh, rows, :], phk[hh, win, :])
            tt = r0 + lax.broadcasted_iota(jnp.int32, (CHUNK, J), 0)
            jj = j0 + lax.broadcasted_iota(jnp.int32, (CHUNK, J), 1)
            start = start_col(r0, CHUNK, e0, e1)
            w = jnp.where(tt - jj >= WINDOW, kap, ee)
            w = jnp.where((tt >= jj) & (jj >= start), w, 0.0)
            nd = dot_nn(w.astype(BF), vaug[kv, win, :])
            if state is not None:
                far = dot_nn(phq[hh, rows, :], state.astype(BF))
                nd = nd + jnp.where(start < j0, far, 0.0)
            rec = 1.0 / nd
            mix = nd * swap(rec)
            nm_ref[hh, rows, :] = jnp.where(low, mix, rec)
            if hh == 0:
                att_ref[rows, :] = mix.astype(BF)
            else:
                att_ref[rows, :] = jnp.where(low, att_ref[rows, :].astype(F32), swap(mix)).astype(BF)
            if r0 + CHUNK < T:
                state = next_state(state, phk, vaug, hh, kv, r0, j0, e0, e1)


def next_state(state, phk, vaug, hh, kv, r0, j0, e0, e1):
    n = r0 + CHUNK - BACK - j0
    nstart = start_of(r0 + CHUNK, e0, e1)
    jc = j0 + lax.broadcasted_iota(jnp.int32, (n, 1), 0)
    new = jnp.where(jc >= nstart, phk[hh, pl.ds(j0, n), :].astype(F32), 0.0).astype(BF)
    add = dot_tn(new, vaug[kv, pl.ds(j0, n), :])
    if state is None:
        return add
    return jnp.where(nstart < j0, state, 0.0) + add


def split2(x):
    hi = x.astype(BF)
    return hi, (x - hi.astype(F32)).astype(BF)


def bwd_kernel(e_ref, c_ref, q_ref, k_ref, v_ref, cos_ref, sin_ref, mq_ref, mk_ref, mqt_ref, mkt_ref,
               nm_ref, da_ref, dq_ref, dk_ref, dv_ref, gq_ref, gk_ref, st_ref,
               kaug, vaug, dkacc, dvacc, qaug, fq, fk, phq, phk, states, gvec, dpq, dpk, dqa, dva, dka, *, rep):
    T = q_ref.shape[0]
    e0, e1 = e_ref[0], e_ref[1]
    p = pl.program_id(0)

    @pl.when(p == 0)
    def _():
        prep_keys(k_ref, v_ref, cos_ref, sin_ref, kaug, vaug, True, e0, e1)
        dkacc[...] = jnp.zeros_like(dkacc)
        dvacc[...] = jnp.zeros_like(dvacc)

    kv = (2 * p) // rep
    ones = half_ones()
    low = lanes(CHUNK) < 64
    lane = lanes(CHUNK)

    def head(hh, _):
        odd = hh == 1
        c = c_ref[2 * p + hh]
        state = None
        for n, r0 in enumerate(range(0, T, CHUNK)):
            rows = pl.ds(r0, CHUNK)
            q = q_ref[rows, :].astype(F32) * (LOG2E / 8.0)
            qr = q * cos_ref[rows, :] + spin(q) * sin_ref[rows, :]
            first, second = prep_query(qr, odd, True, r0, e0, e1)
            qaug[rows, 0:128] = first
            qaug[rows, 128:256] = second
            f = features(qaug[rows, :], mq_ref[hh], ones)
            fq[rows, :] = f
            phq[0, rows, :] = (f * c).astype(BF)
            f = features(kaug[kv, rows, :], mk_ref[hh], ones)
            fk[rows, :] = f
            phk[0, rows, :] = f.astype(BF)
            j0 = max(r0 - BACK, 0)
            if state is not None:
                states[n] = state.astype(BF)
            if r0 + CHUNK < T:
                state = next_state(state, phk, vaug, 0, kv, r0, j0, e0, e1)
        dpk[...] = jnp.zeros_like(dpk)
        dva[...] = jnp.zeros_like(dva)
        dka[...] = jnp.zeros_like(dka)
        square = jnp.zeros((1, 128), F32)
        for n, r0 in enumerate(range(0, T, CHUNK)):
            rows = pl.ds(r0, CHUNK)
            wide = pl.ds(0, r0 + CHUNK)
            diag = pl.ds(r0, CHUNK)
            tcol = r0 + lax.broadcasted_iota(jnp.int32, (CHUNK, 1), 0)
            start = start_of(tcol, e0, e1)
            full = r0 + CHUNK
            s = dot_nt(qaug[rows, :], kaug[kv, wide, :])
            tt = r0 + lax.broadcasted_iota(jnp.int32, (CHUNK, full), 0)
            jj = lax.broadcasted_iota(jnp.int32, (CHUNK, full), 1)
            ee = jnp.exp2(s)
            ee = jnp.where(tt >= jj, ee, 0.0)
            eb = ee.astype(BF)
            nd = dot_nn(eb, vaug[kv, wide, :])
            rec = 1.0 / nd
            soft = nd * swap(rec)
            soft = jnp.where(low, soft, swap(soft))
            srec = jnp.where(low, swap(rec), rec)
            nm = nm_ref[hh, rows, :]
            other = swap(nm)
            mix = jnp.where(low, nm, other)
            mrec = jnp.where(low, other, nm)
            delta = jnp.where(tcol < e1, mix - soft, 0.0)
            square = square + jnp.sum(delta * delta, axis=0, keepdims=True)
            g = twin(da_ref[rows, :], odd) + delta
            gd = -0.5 * jnp.sum(g * mix, axis=1, keepdims=True)
            gx = jnp.where(low, g, jnp.where(lane == 64, gd, 0.0)) * mrec
            hd = 0.5 * jnp.sum(delta * soft, axis=1, keepdims=True)
            hx = jnp.where(low, -delta, jnp.where(lane == 64, hd, 0.0)) * srec
            ghi, glo = split2(gx)
            hhi, hlo = split2(hx)
            gvec[rows, :] = ghi
            va = vaug[kv, wide, :]
            r = dot_nt(jnp.concatenate([hhi, hlo], axis=1), jnp.concatenate([va, va], axis=1))
            j0 = max(r0 - BACK, 0)
            J = full - j0
            win = pl.ds(j0, J)
            vw = vaug[kv, win, :]
            pw = dot_nt(jnp.concatenate([ghi, glo], axis=1), jnp.concatenate([vw, vw], axis=1))
            kap = dot_nt(phq[0, rows, :], phk[0, win, :])
            tw = r0 + lax.broadcasted_iota(jnp.int32, (CHUNK, J), 0)
            jw = j0 + lax.broadcasted_iota(jnp.int32, (CHUNK, J), 1)
            far = tw - jw >= WINDOW
            live = far & (jw >= start)
            w = jnp.where(far, jnp.where(live, kap, 0.0), ee[:, j0:]).astype(BF)
            dkap = jnp.where(live, pw, 0.0).astype(BF)
            rn = r[:, j0:] + jnp.where(far, 0.0, pw)
            if j0:
                r = jnp.concatenate([r[:, :j0], rn], axis=1)
            else:
                r = rn
            ds = (ee * r).astype(BF)
            dqa[rows, :] = dot_nn(ds, kaug[kv, wide, 0:128])
            dka[wide, :] += dot_tn(ds, qaug[rows, 128:256])
            dva[wide, :] += dot_tn(eb, hhi)
            dva[win, :] += dot_tn(w, ghi)
            df = dot_nn(dkap, phk[0, win, :])
            if n:
                df = df + jnp.where(start < j0, dot_nt(ghi, states[n]), 0.0)
            dpq[rows, :] = df
            dpk[win, :] += dot_tn(dkap, phq[0, rows, :])
        back = None
        for n in reversed(range(T // CHUNK)):
            r0 = n * CHUNK
            j0 = max(r0 - BACK, 0)
            m = r0 + CHUNK - BACK - j0
            if back is not None:
                keys = pl.ds(j0, m)
                nstart = start_of(r0 + CHUNK, e0, e1)
                jc = j0 + lax.broadcasted_iota(jnp.int32, (m, 1), 0)
                bb = back.astype(BF)
                dpk[keys, :] += jnp.where(jc >= nstart, dot_nt(vaug[kv, keys, :], bb), 0.0)
                dva[keys, :] += jnp.where(jc >= nstart, dot_nn(phk[0, keys, :], bb), 0.0)
                back = jnp.where(nstart < j0, back, 0.0)
            if n:
                rows = pl.ds(r0, CHUNK)
                start = start_col(r0, CHUNK, e0, e1)
                pq = jnp.where(start < j0, phq[0, rows, :].astype(F32), 0.0).astype(BF)
                add = dot_tn(pq, gvec[rows, :])
                back = add if back is None else back + add
        window = jnp.zeros((1, 128), F32)
        dmq = jnp.zeros((128, 128), F32)
        dmk = jnp.zeros((128, 128), F32)
        ones2 = jnp.concatenate([ones, ones], axis=0)
        for r0 in range(0, T, CHUNK):
            rows = pl.ds(r0, CHUNK)
            f = fq[rows, :]
            prod = f * (dpq[rows, :] * c)
            window = window + jnp.sum(prod, axis=0, keepdims=True)
            hi, lo = split2(prod)
            dp = (prod - f * dot_nn(jnp.concatenate([hi, lo], axis=1), ones2)).astype(BF)
            dmq = dmq + dot_tn(qaug[rows, 128:256], dp)
            dq = dqa[rows, :] * 0.125 + dot_nn(dp, mqt_ref[hh])
            dq = dq * cos_ref[rows, :] - spin(dq) * sin_ref[rows, :]
            keep = low if isinstance(hh, int) and hh == 0 else (low == (hh == 0))
            dq_ref[rows, :] = jnp.where(keep, dq, dq_ref[rows, :].astype(F32)).astype(BF)
            f = fk[rows, :]
            prod = f * dpk[rows, :]
            hi, lo = split2(prod)
            dp = (prod - f * dot_nn(jnp.concatenate([hi, lo], axis=1), ones2)).astype(BF)
            dmk = dmk + dot_tn(kaug[kv, rows, 0:128], dp)
            dkacc[kv, rows, :] += dka[rows, :] * LN2 + dot_nn(dp, mkt_ref[hh])
            dvacc[kv, rows, :] += dva[rows, :]
        dmq = (dmq - swap(dmq)) * (8.0 * LN2)
        dmk = dmk - swap(dmk)
        gq_ref[hh] = dmq[0:64, 0:64]
        gk_ref[hh] = dmk[0:64, 0:64]
        st_ref[hh, 0:1, :] = square
        st_ref[hh, 1:2, :] = window
        return 0

    lax.fori_loop(0, 2, head, 0)

    @pl.when(p == pl.num_programs(0) - 1)
    def _():
        for r0 in range(0, T, CHUNK):
            rows = pl.ds(r0, CHUNK)
            dk = jnp.where(low, dkacc[0, rows, :], swap(dkacc[1, rows, :]))
            dk_ref[rows, :] = (dk * cos_ref[rows, :] - spin(dk) * sin_ref[rows, :]).astype(BF)
            dv_ref[rows, :] = jnp.where(low, dvacc[0, rows, :], swap(dvacc[1, rows, :])).astype(BF)


def rotary_tables(position):
    freq = 500000.0 ** (-2.0 * jnp.arange(32, dtype=F32) / 64)
    angle = position.astype(F32)[:, None] * freq[None, :]
    cosine, sine = jnp.cos(angle), jnp.sin(angle)
    return jnp.concatenate([cosine] * 4, axis=1), jnp.concatenate([-sine, sine] * 2, axis=1)


def pack_maps(maps, scale, keys):
    both = jnp.concatenate([maps, -maps], axis=2) * scale
    hi = lax.reduce_precision(both, 8, 7)
    lo = both - hi
    parts = [hi, lo, hi] if keys else [hi, hi, lo]
    return jnp.concatenate([*parts, jnp.zeros_like(lo)], axis=1).astype(BF)


def flip_maps(maps):
    both = jnp.swapaxes(jnp.concatenate([maps, -maps], axis=2), 1, 2)
    return jnp.concatenate([both, both], axis=2).astype(BF)


def attention_fwd(ends, cees, q, k, v, cosine, sine, mq, mk):
    T, H = q.shape[0], q.shape[1] // HD
    rep = 4
    full = lambda shape: pl.BlockSpec(shape, lambda p: (0,) * len(shape))
    pair = pl.BlockSpec((T, 128), lambda p: (0, p))
    heads = lambda *shape: pl.BlockSpec((2, *shape), lambda p: (p, 0, 0))
    smem = pl.BlockSpec(memory_space=pltpu.SMEM)
    return pl.pallas_call(
        functools.partial(fwd_kernel, rep=rep),
        grid=(H // 2,),
        in_specs=[smem, smem, pair, full((T, 128)), full((T, 128)), full((T, 128)), full((T, 128)),
                  heads(256, 128), heads(256, 128)],
        out_specs=[pair, heads(T, 128)],
        out_shape=[jax.ShapeDtypeStruct((T, H * HD), BF), jax.ShapeDtypeStruct((H, T, 128), F32)],
        scratch_shapes=[pltpu.VMEM((2, T, 256), BF), pltpu.VMEM((2, T, 128), BF), pltpu.VMEM((2, T, 256), BF),
                        pltpu.VMEM((2, T, 128), BF), pltpu.VMEM((2, T, 128), BF)],
        compiler_params=pltpu.CompilerParams(vmem_limit_bytes=48 * 2**20),
        cost_estimate=pl.CostEstimate(flops=H * 8 * 2**30, bytes_accessed=16 * 2**20, transcendentals=0),
        name="mix_forward",
    )(ends, cees, q, k, v, cosine, sine, mq, mk)


def attention_bwd(ends, cees, q, k, v, cosine, sine, mq, mk, mqt, mkt, nm, da):
    T, H = q.shape[0], q.shape[1] // HD
    rep = 4
    full = lambda shape: pl.BlockSpec(shape, lambda p: (0,) * len(shape))
    pair = pl.BlockSpec((T, 128), lambda p: (0, p))
    heads = lambda *shape: pl.BlockSpec((2, *shape), lambda p: (p, 0, 0))
    smem = pl.BlockSpec(memory_space=pltpu.SMEM)
    wide = full((T, 128))
    f32buf = pltpu.VMEM((T, 128), F32)
    return pl.pallas_call(
        functools.partial(bwd_kernel, rep=rep),
        grid=(H // 2,),
        in_specs=[smem, smem, pair, wide, wide, wide, wide, heads(256, 128), heads(256, 128),
                  heads(128, 128), heads(128, 128), heads(T, 128), pair],
        out_specs=[pair, wide, wide, heads(64, 64), heads(64, 64), heads(8, 128)],
        out_shape=[jax.ShapeDtypeStruct((T, H * HD), BF), jax.ShapeDtypeStruct((T, 128), BF),
                   jax.ShapeDtypeStruct((T, 128), BF), jax.ShapeDtypeStruct((H, 64, 64), F32),
                   jax.ShapeDtypeStruct((H, 64, 64), F32), jax.ShapeDtypeStruct((H, 8, 128), F32)],
        scratch_shapes=[pltpu.VMEM((2, T, 256), BF), pltpu.VMEM((2, T, 128), BF),
                        pltpu.VMEM((2, T, 128), F32), pltpu.VMEM((2, T, 128), F32),
                        pltpu.VMEM((T, 256), BF), f32buf, f32buf,
                        pltpu.VMEM((1, T, 128), BF), pltpu.VMEM((1, T, 128), BF),
                        pltpu.VMEM((T // CHUNK, 128, 128), BF), pltpu.VMEM((T, 128), BF),
                        f32buf, f32buf, f32buf, f32buf, f32buf],
        compiler_params=pltpu.CompilerParams(vmem_limit_bytes=56 * 2**20),
        cost_estimate=pl.CostEstimate(flops=H * 32 * 2**30, bytes_accessed=24 * 2**20, transcendentals=0),
        name="mix_backward",
    )(ends, cees, q, k, v, cosine, sine, mq, mk, mqt, mkt, nm, da)

ASKER_COUNT = 32
norm_eps = 1e-05
factored_multiplier = 2.0


def plain_contract(left, right):
    return jnp.dot(left, right, preferred_element_type=jnp.float32)


def transposed_right_product(left, right):
    return dot_nt(left, right)


def flipped_first_contract(left, right):
    return dot_tn(left, right)


def rms_scale(values):
    return lax.rsqrt(jnp.mean(values * values, axis=-1, keepdims=True) + norm_eps)


def norm_back(values, scale_in, gain_in, grad_normed):
    weighted = grad_normed * gain_in
    grad_values = scale_in * weighted - values * (scale_in * scale_in * scale_in) * jnp.mean(
        weighted * values, axis=-1, keepdims=True
    )
    grad_gain = jnp.sum(grad_normed * values * scale_in, axis=0)
    return (grad_values, grad_gain)


def local(
    layer_tokens,
    sequence_extents,
    loss_sensitivity,
    mixing_rms_gain,
    asker_dense_map,
    lookup_dense_map,
    content_dense_map,
    shrink_map_asker,
    grow_map_asker,
    shrink_map_lookup,
    grow_map_lookup,
    shrink_map_content,
    grow_map_content,
    asker_feature_maps,
    lookup_feature_maps,
    local_portion_logit,
    emitted_mixing_map,
    emitted_shrink_map,
    emitted_grow_map,
    feedforward_rms_gain,
    gating_dense_map,
    widen_dense_map,
    shrink_dense_map,
):
    rows_dev = layer_tokens.shape[0]
    group_rows = rows_dev * lax.axis_size("mp")
    tokens_all = group_rows * lax.axis_size("batch")
    heads_dev = asker_dense_map.shape[1] // HD
    key_heads = lookup_dense_map.shape[1] // HD
    rank_width = shrink_map_asker.shape[1]
    first_end = sequence_extents[0, 0]
    second_end = first_end + sequence_extents[0, 1]
    ends = jnp.stack([first_end, second_end])
    places = jnp.arange(group_rows, dtype=jnp.int32)
    position = places - start_of(places, first_end, second_end)
    cosine, sine = rotary_tables(position)
    residual_in = layer_tokens.astype(jnp.float32)
    scale_one = rms_scale(residual_in)
    normalized_input = (residual_in * scale_one * mixing_rms_gain).astype(jnp.bfloat16)
    collected_rows = lax.all_gather(normalized_input, "mp", axis=0, tiled=True)
    cot_rows = lax.all_gather(loss_sensitivity, "mp", axis=0, tiled=True)

    q_cols, k_cols = heads_dev * HD, key_heads * HD
    dense_all = jnp.concatenate(
        [asker_dense_map, lookup_dense_map, content_dense_map], axis=1
    )
    a_all_wide = jnp.concatenate([shrink_map_asker, shrink_map_lookup, shrink_map_content], axis=1)
    grow_all = jnp.concatenate(
        [
            jnp.pad(grow_map_asker, ((0, 0), (0, 2 * k_cols))),
            jnp.pad(grow_map_lookup, ((0, 0), (q_cols, k_cols))),
            jnp.pad(grow_map_content, ((0, 0), (q_cols + k_cols, 0))),
        ],
        axis=0,
    )
    middle_rows = plain_contract(collected_rows, a_all_wide).astype(jnp.bfloat16)
    projected = (
        plain_contract(collected_rows, dense_all)
        + factored_multiplier * plain_contract(middle_rows, grow_all)
    ).astype(jnp.bfloat16)
    query_proj = projected[:, :q_cols]
    spare = max(0, 128 - k_cols)
    key_proj = jnp.pad(projected[:, q_cols : q_cols + k_cols], ((0, 0), (0, spare)))
    value_proj = jnp.pad(projected[:, q_cols + k_cols :], ((0, 0), (0, spare)))
    cees = jnp.exp(-local_portion_logit)
    attention_args = (
        ends,
        cees,
        query_proj,
        key_proj,
        value_proj,
        cosine,
        sine,
        pack_maps(asker_feature_maps, 8.0, False),
        pack_maps(lookup_feature_maps, LOG2E, True),
    )
    mixing_outcome, mixed_kept = attention_fwd(*attention_args)
    emitted_inner_tokens = plain_contract(mixing_outcome, emitted_shrink_map).astype(jnp.bfloat16)
    factored_path = lax.psum_scatter(
        (
            plain_contract(mixing_outcome, emitted_mixing_map)
            + factored_multiplier * plain_contract(emitted_inner_tokens, emitted_grow_map)
        ).astype(jnp.bfloat16),
        "mp",
        scatter_dimension=0,
        tiled=True,
    ).astype(jnp.float32)
    hidden = residual_in + factored_path
    scale_two = rms_scale(hidden)
    normed_two = (hidden * scale_two * feedforward_rms_gain).astype(jnp.bfloat16)
    gathered_two = lax.all_gather(normed_two, "mp", axis=0, tiled=True)
    gate_proj = plain_contract(gathered_two, gating_dense_map)
    up_proj = plain_contract(gathered_two, widen_dense_map)
    gate_sig = jax.nn.sigmoid(gate_proj)
    active = (gate_proj * gate_sig * up_proj).astype(jnp.bfloat16)
    mlp_part = lax.psum_scatter(
        plain_contract(active, shrink_dense_map).astype(jnp.bfloat16),
        "mp",
        scatter_dimension=0,
        tiled=True,
    ).astype(jnp.float32)
    output = (hidden + mlp_part).astype(jnp.bfloat16)
    d_active = transposed_right_product(cot_rows, shrink_dense_map)
    grad_w_down = flipped_first_contract(active, cot_rows)
    d_gate = (d_active * up_proj * gate_sig * (1.0 + gate_proj * (1.0 - gate_sig))).astype(
        jnp.bfloat16
    )
    d_up = (d_active * gate_proj * gate_sig).astype(jnp.bfloat16)
    grad_w_gate = flipped_first_contract(gathered_two, d_gate)
    grad_w_up = flipped_first_contract(gathered_two, d_up)
    d_normed_two = lax.psum_scatter(
        (
            transposed_right_product(d_gate, gating_dense_map)
            + transposed_right_product(d_up, widen_dense_map)
        ).astype(jnp.bfloat16),
        "mp",
        scatter_dimension=0,
        tiled=True,
    ).astype(jnp.float32)
    d_hidden_norm, grad_norm_two = norm_back(hidden, scale_two, feedforward_rms_gain, d_normed_two)
    d_hidden = loss_sensitivity.astype(jnp.float32) + d_hidden_norm
    factored_path_derivative = lax.all_gather(
        d_hidden.astype(jnp.bfloat16), "mp", axis=0, tiled=True
    )
    grad_w_out = flipped_first_contract(mixing_outcome, factored_path_derivative)
    emitted_inner_derivative = (
        factored_multiplier * transposed_right_product(factored_path_derivative, emitted_grow_map)
    ).astype(jnp.bfloat16)
    grad_a_out = flipped_first_contract(mixing_outcome, emitted_inner_derivative)
    emitted_grow_derivative = factored_multiplier * flipped_first_contract(
        emitted_inner_tokens, factored_path_derivative
    )
    d_attended = transposed_right_product(
        factored_path_derivative, emitted_mixing_map
    ) + transposed_right_product(emitted_inner_derivative, emitted_shrink_map)
    (
        query_lowrank_gradient,
        key_lowrank_gradient,
        value_lowrank_gradient,
        grad_query_maps,
        grad_key_maps,
        kept_sums,
    ) = attention_bwd(
        *attention_args,
        flip_maps(asker_feature_maps),
        flip_maps(lookup_feature_maps),
        mixed_kept,
        d_attended,
    )
    teacher_sq = jnp.sum(kept_sums[:, 0, :HD])
    grad_window = -jnp.sum(kept_sums[:, 1, :], axis=1)
    projected_gradient = jnp.concatenate(
        [
            query_lowrank_gradient,
            key_lowrank_gradient[:, :k_cols],
            value_lowrank_gradient[:, :k_cols],
        ],
        axis=1,
    )
    grad_w_all = flipped_first_contract(collected_rows, projected_gradient)
    grad_w_query = grad_w_all[:, :q_cols]
    grad_w_key = grad_w_all[:, q_cols : q_cols + k_cols]
    grad_w_value = grad_w_all[:, q_cols + k_cols :]
    grow_all_derivative = factored_multiplier * flipped_first_contract(
        middle_rows, projected_gradient
    )
    asker_grow_derivative = grow_all_derivative[:rank_width, :q_cols]
    lookup_grow_derivative = grow_all_derivative[
        rank_width : 2 * rank_width, q_cols : q_cols + k_cols
    ]
    content_grow_derivative = grow_all_derivative[2 * rank_width :, q_cols + k_cols :]
    combined_middle_gradient = (
        factored_multiplier * transposed_right_product(projected_gradient, grow_all)
    ).astype(jnp.bfloat16)
    grad_a_all = flipped_first_contract(collected_rows, combined_middle_gradient)
    grad_a_query = grad_a_all[:, :rank_width]
    grad_a_key = grad_a_all[:, rank_width : 2 * rank_width]
    grad_a_value = grad_a_all[:, 2 * rank_width :]
    through_weights = transposed_right_product(projected_gradient, dense_all)
    d_normed = lax.psum_scatter(
        (through_weights + transposed_right_product(combined_middle_gradient, a_all_wide)).astype(
            jnp.bfloat16
        ),
        "mp",
        scatter_dimension=0,
        tiled=True,
    ).astype(jnp.float32)
    d_inputs_norm, grad_norm_one = norm_back(residual_in, scale_one, mixing_rms_gain, d_normed)
    input_grad = (d_hidden + d_inputs_norm).astype(jnp.bfloat16)
    (
        grad_norm_one,
        grad_norm_two,
        grad_a_query,
        grad_a_key,
        grad_a_value,
        emitted_grow_derivative,
        teacher_sq,
    ) = lax.psum(
        (
            grad_norm_one,
            grad_norm_two,
            grad_a_query,
            grad_a_key,
            grad_a_value,
            emitted_grow_derivative,
            teacher_sq,
        ),
        ("batch", "mp"),
    )
    (
        grad_w_query,
        grad_w_key,
        grad_w_value,
        asker_grow_derivative,
        lookup_grow_derivative,
        content_grow_derivative,
        grad_query_maps,
        grad_key_maps,
        grad_window,
        grad_w_out,
        grad_a_out,
        grad_w_gate,
        grad_w_up,
        grad_w_down,
    ) = (
        lax.psum(grad_w_query.astype(jnp.bfloat16), "batch").astype(jnp.float32),
        lax.psum(grad_w_key.astype(jnp.bfloat16), "batch").astype(jnp.float32),
        lax.psum(grad_w_value.astype(jnp.bfloat16), "batch").astype(jnp.float32),
        lax.psum(asker_grow_derivative.astype(jnp.bfloat16), "batch").astype(jnp.float32),
        lax.psum(lookup_grow_derivative.astype(jnp.bfloat16), "batch").astype(jnp.float32),
        lax.psum(content_grow_derivative.astype(jnp.bfloat16), "batch").astype(jnp.float32),
        lax.psum(grad_query_maps.astype(jnp.bfloat16), "batch").astype(jnp.float32),
        lax.psum(grad_key_maps.astype(jnp.bfloat16), "batch").astype(jnp.float32),
        lax.psum(grad_window.astype(jnp.bfloat16), "batch").astype(jnp.float32),
        lax.psum(grad_w_out.astype(jnp.bfloat16), "batch").astype(jnp.float32),
        lax.psum(grad_a_out.astype(jnp.bfloat16), "batch").astype(jnp.float32),
        lax.psum(grad_w_gate.astype(jnp.bfloat16), "batch").astype(jnp.float32),
        lax.psum(grad_w_up.astype(jnp.bfloat16), "batch").astype(jnp.float32),
        lax.psum(grad_w_down.astype(jnp.bfloat16), "batch").astype(jnp.float32),
    )
    teacher_mse = teacher_sq / float(tokens_all * ASKER_COUNT * HD)
    return (
        output,
        input_grad,
        grad_norm_one,
        grad_w_query,
        grad_w_key,
        grad_w_value,
        grad_a_query,
        asker_grow_derivative,
        grad_a_key,
        lookup_grow_derivative,
        grad_a_value,
        content_grow_derivative,
        grad_query_maps,
        grad_key_maps,
        grad_window,
        grad_w_out,
        grad_a_out,
        emitted_grow_derivative,
        grad_norm_two,
        grad_w_gate,
        grad_w_up,
        grad_w_down,
        teacher_mse,
    )


def solution(mesh):
    return jax.shard_map(
        local,
        mesh=mesh,
        in_specs=(
            P(("batch", "mp"), None),
            P("batch", None),
            P(("batch", "mp"), None),
            P(),
            P(None, "mp"),
            P(None, "mp"),
            P(None, "mp"),
            P(),
            P(None, "mp"),
            P(),
            P(None, "mp"),
            P(),
            P(None, "mp"),
            P("mp", None, None),
            P("mp", None, None),
            P("mp"),
            P("mp", None),
            P("mp", None),
            P(),
            P(),
            P(None, "mp"),
            P(None, "mp"),
            P("mp", None),
        ),
        out_specs=(
            P(("batch", "mp"), None),
            P(("batch", "mp"), None),
            P(),
            P(None, "mp"),
            P(None, "mp"),
            P(None, "mp"),
            P(),
            P(None, "mp"),
            P(),
            P(None, "mp"),
            P(),
            P(None, "mp"),
            P("mp", None, None),
            P("mp", None, None),
            P("mp"),
            P("mp", None),
            P("mp", None),
            P(),
            P(),
            P(None, "mp"),
            P(None, "mp"),
            P("mp", None),
            P(),
        ),
        check_vma=False,
    )
```

```python
import functools
import math
import jax
import jax.numpy as jnp
from jax import lax
from jax.experimental import pallas as pl
from jax.experimental.pallas import tpu as pltpu
from jax.sharding import PartitionSpec as P

HD = 64
WINDOW = 64
CHUNK = 256
BACK = 128
LOG2E = math.log2(math.e)
LN2 = math.log(2.0)
BIG = 16384.0
F32 = jnp.float32
BF = jnp.bfloat16


def dot_nn(a, b):
    return lax.dot_general(a, b, (((1,), (0,)), ((), ())), preferred_element_type=F32)


def dot_nt(a, b):
    return lax.dot_general(a, b, (((1,), (1,)), ((), ())), preferred_element_type=F32)


def dot_tn(a, b):
    return lax.dot_general(a, b, (((0,), (0,)), ((), ())), preferred_element_type=F32)


def lanes(rows):
    return lax.broadcasted_iota(jnp.int32, (rows, 128), 1)


def swap(x):
    return pltpu.roll(x, 64, 1)


def spin(x):
    lane = lanes(x.shape[0])
    return jnp.where((lane & 63) < 32, pltpu.roll(x, 96, 1), pltpu.roll(x, 32, 1))


def twin(x, odd):
    low = lanes(x.shape[0]) < 64
    other = swap(x)
    return jnp.where(low != odd, x, other)


def half_ones():
    r = lax.broadcasted_iota(jnp.int32, (128, 128), 0)
    c = lax.broadcasted_iota(jnp.int32, (128, 128), 1)
    return ((r < 64) == (c < 64)).astype(BF)


def start_of(t, e0, e1):
    return jnp.where(t >= e1, e1, jnp.where(t >= e0, e0, 0))


def start_col(r0, rows, e0, e1):
    t = r0 + lax.broadcasted_iota(jnp.int32, (rows, 1), 0)
    return start_of(t, e0, e1)


def prep_keys(k_ref, v_ref, cos_ref, sin_ref, kaug, vaug, seg, e0, e1, heads=(0, 1)):
    T = k_ref.shape[0]
    for r0 in range(0, T, CHUNK):
        rows = pl.ds(r0, CHUNK)
        k = k_ref[rows, :].astype(F32)
        v = v_ref[rows, :].astype(F32)
        kr = k * cos_ref[rows, :] + spin(k) * sin_ref[rows, :]
        lane = lanes(CHUNK)
        low = lane < 64
        if seg:
            t = r0 + lax.broadcasted_iota(jnp.int32, (CHUNK, 1), 0)
            mine = (t >= e0).astype(jnp.int32) + (t >= e1).astype(jnp.int32) + 64
            tail = jnp.where((lane < 67) & (lane != mine), -BIG, 0.0)
        else:
            tail = 0.0
        for at, kv in enumerate(heads):
            x = twin(kr, kv == 1)
            hi = x.astype(BF)
            lo = x - hi.astype(F32)
            kaug[at, rows, 0:128] = hi
            kaug[at, rows, 128:256] = jnp.where(low, lo, tail).astype(BF)
            vaug[at, rows, :] = jnp.where(low, v if kv == 0 else swap(v), 1.0).astype(BF)


def prep_query(qr, odd, seg, r0, e0, e1):
    x = twin(qr, odd)
    hi = x.astype(BF)
    lo = (x - hi.astype(F32)).astype(BF)
    lane = lanes(x.shape[0])
    low = lane < 64
    first = jnp.where(low, hi, lo)
    second = hi
    if seg:
        t = r0 + lax.broadcasted_iota(jnp.int32, (x.shape[0], 1), 0)
        mine = (t >= e0).astype(jnp.int32) + (t >= e1).astype(jnp.int32) + 64
        second = jnp.where(low, hi.astype(F32), jnp.where(lane == mine, 1.0, 0.0)).astype(BF)
    return first, second


def features(aug, maps, ones):
    p = jnp.exp2(dot_nn(aug, maps))
    return p / dot_nn(p.astype(BF), ones)


def fwd_kernel(e_ref, c_ref, q_ref, k_ref, v_ref, cos_ref, sin_ref, mq_ref, mk_ref,
               att_ref, nm_ref, kaug, vaug, qaug, phq, phk, *, rep):
    T = q_ref.shape[0]
    e0, e1 = e_ref[0], e_ref[1]
    p = pl.program_id(0)

    @pl.when(p == 0)
    def _():
        prep_keys(k_ref, v_ref, cos_ref, sin_ref, kaug, vaug, False, e0, e1)

    kv = (2 * p) // rep
    ones = half_ones()
    low = lanes(CHUNK) < 64
    for r0 in range(0, T, CHUNK):
        rows = pl.ds(r0, CHUNK)
        q = q_ref[rows, :].astype(F32) * (LOG2E / 8.0)
        qr = q * cos_ref[rows, :] + spin(q) * sin_ref[rows, :]
        for hh in range(2):
            first, second = prep_query(qr, hh == 1, False, r0, e0, e1)
            qaug[hh, rows, 0:128] = first
            qaug[hh, rows, 128:256] = second
            c = c_ref[2 * p + hh]
            phq[hh, rows, :] = (features(qaug[hh, rows, :], mq_ref[hh], ones) * c).astype(BF)
            phk[hh, rows, :] = features(kaug[kv, rows, :], mk_ref[hh], ones).astype(BF)
    for hh in range(2):
        state = None
        for r0 in range(0, T, CHUNK):
            rows = pl.ds(r0, CHUNK)
            j0 = max(r0 - BACK, 0)
            J = r0 + CHUNK - j0
            win = pl.ds(j0, J)
            ee = jnp.exp2(dot_nt(qaug[hh, rows, :], kaug[kv, win, :]))
            kap = dot_nt(phq[hh, rows, :], phk[hh, win, :])
            tt = r0 + lax.broadcasted_iota(jnp.int32, (CHUNK, J), 0)
            jj = j0 + lax.broadcasted_iota(jnp.int32, (CHUNK, J), 1)
            start = start_col(r0, CHUNK, e0, e1)
            w = jnp.where(tt - jj >= WINDOW, kap, ee)
            w = jnp.where((tt >= jj) & (jj >= start), w, 0.0)
            nd = dot_nn(w.astype(BF), vaug[kv, win, :])
            if state is not None:
                far = dot_nn(phq[hh, rows, :], state.astype(BF))
                nd = nd + jnp.where(start < j0, far, 0.0)
            rec = 1.0 / nd
            mix = nd * swap(rec)
            nm_ref[hh, rows, :] = jnp.where(low, mix, rec)
            if hh == 0:
                att_ref[rows, :] = mix.astype(BF)
            else:
                att_ref[rows, :] = jnp.where(low, att_ref[rows, :].astype(F32), swap(mix)).astype(BF)
            if r0 + CHUNK < T:
                state = next_state(state, phk, vaug, hh, kv, r0, j0, e0, e1)


def next_state(state, phk, vaug, hh, kv, r0, j0, e0, e1):
    n = r0 + CHUNK - BACK - j0
    nstart = start_of(r0 + CHUNK, e0, e1)
    jc = j0 + lax.broadcasted_iota(jnp.int32, (n, 1), 0)
    new = jnp.where(jc >= nstart, phk[hh, pl.ds(j0, n), :].astype(F32), 0.0).astype(BF)
    add = dot_tn(new, vaug[kv, pl.ds(j0, n), :])
    if state is None:
        return add
    return jnp.where(nstart < j0, state, 0.0) + add


def split2(x):
    hi = x.astype(BF)
    return hi, (x - hi.astype(F32)).astype(BF)


def bwd_kernel(e_ref, c_ref, q_ref, k_ref, v_ref, cos_ref, sin_ref, mq_ref, mk_ref, mqt_ref, mkt_ref,
               nm_ref, da_ref, dq_ref, dk_ref, dv_ref, gq_ref, gk_ref, st_ref,
               kaug, vaug, qaug, fq, fk, phq, phk, states, gvec, dpq, dpk, dqa, dva, dka, *, pair, kv):
    T = q_ref.shape[0]
    e0, e1 = e_ref[0], e_ref[1]
    prep_keys(k_ref, v_ref, cos_ref, sin_ref, kaug, vaug, True, e0, e1, (kv,))
    dk_ref[...] = jnp.zeros_like(dk_ref)
    dv_ref[...] = jnp.zeros_like(dv_ref)
    ones = half_ones()
    low = lanes(CHUNK) < 64
    lane = lanes(CHUNK)

    def head(hh, _):
        odd = hh == 1
        c = c_ref[2 * pair + hh]
        state = None
        for n, r0 in enumerate(range(0, T, CHUNK)):
            rows = pl.ds(r0, CHUNK)
            q = q_ref[rows, :].astype(F32) * (LOG2E / 8.0)
            qr = q * cos_ref[rows, :] + spin(q) * sin_ref[rows, :]
            first, second = prep_query(qr, odd, True, r0, e0, e1)
            qaug[rows, 0:128] = first
            qaug[rows, 128:256] = second
            f = features(qaug[rows, :], mq_ref[hh], ones)
            fq[rows, :] = f
            phq[0, rows, :] = (f * c).astype(BF)
            f = features(kaug[0, rows, :], mk_ref[hh], ones)
            fk[rows, :] = f
            phk[0, rows, :] = f.astype(BF)
            j0 = max(r0 - BACK, 0)
            if state is not None:
                states[n] = state.astype(BF)
            if r0 + CHUNK < T:
                state = next_state(state, phk, vaug, 0, 0, r0, j0, e0, e1)
        dpk[...] = jnp.zeros_like(dpk)
        dva[...] = jnp.zeros_like(dva)
        dka[...] = jnp.zeros_like(dka)
        square = jnp.zeros((1, 128), F32)
        for n, r0 in enumerate(range(0, T, CHUNK)):
            rows = pl.ds(r0, CHUNK)
            wide = pl.ds(0, r0 + CHUNK)
            diag = pl.ds(r0, CHUNK)
            tcol = r0 + lax.broadcasted_iota(jnp.int32, (CHUNK, 1), 0)
            start = start_of(tcol, e0, e1)
            full = r0 + CHUNK
            s = dot_nt(qaug[rows, :], kaug[0, wide, :])
            tt = r0 + lax.broadcasted_iota(jnp.int32, (CHUNK, full), 0)
            jj = lax.broadcasted_iota(jnp.int32, (CHUNK, full), 1)
            ee = jnp.exp2(s)
            ee = jnp.where(tt >= jj, ee, 0.0)
            eb = ee.astype(BF)
            nd = dot_nn(eb, vaug[0, wide, :])
            rec = 1.0 / nd
            soft = nd * swap(rec)
            soft = jnp.where(low, soft, swap(soft))
            srec = jnp.where(low, swap(rec), rec)
            nm = nm_ref[hh, rows, :]
            other = swap(nm)
            mix = jnp.where(low, nm, other)
            mrec = jnp.where(low, other, nm)
            delta = jnp.where(tcol < e1, mix - soft, 0.0)
            square = square + jnp.sum(delta * delta, axis=0, keepdims=True)
            g = twin(da_ref[rows, :], odd) + delta
            gd = -0.5 * jnp.sum(g * mix, axis=1, keepdims=True)
            gx = jnp.where(low, g, jnp.where(lane == 64, gd, 0.0)) * mrec
            hd = 0.5 * jnp.sum(delta * soft, axis=1, keepdims=True)
            hx = jnp.where(low, -delta, jnp.where(lane == 64, hd, 0.0)) * srec
            ghi, glo = split2(gx)
            hhi, hlo = split2(hx)
            gvec[rows, :] = ghi
            va = vaug[0, wide, :]
            r = dot_nt(jnp.concatenate([hhi, hlo], axis=1), jnp.concatenate([va, va], axis=1))
            j0 = max(r0 - BACK, 0)
            J = full - j0
            win = pl.ds(j0, J)
            vw = vaug[0, win, :]
            pw = dot_nt(jnp.concatenate([ghi, glo], axis=1), jnp.concatenate([vw, vw], axis=1))
            kap = dot_nt(phq[0, rows, :], phk[0, win, :])
            tw = r0 + lax.broadcasted_iota(jnp.int32, (CHUNK, J), 0)
            jw = j0 + lax.broadcasted_iota(jnp.int32, (CHUNK, J), 1)
            far = tw - jw >= WINDOW
            live = far & (jw >= start)
            w = jnp.where(far, jnp.where(live, kap, 0.0), ee[:, j0:]).astype(BF)
            dkap = jnp.where(live, pw, 0.0).astype(BF)
            rn = r[:, j0:] + jnp.where(far, 0.0, pw)
            if j0:
                r = jnp.concatenate([r[:, :j0], rn], axis=1)
            else:
                r = rn
            ds = (ee * r).astype(BF)
            dqa[rows, :] = dot_nn(ds, kaug[0, wide, 0:128])
            dka[wide, :] += dot_tn(ds, qaug[rows, 128:256])
            dva[wide, :] += dot_tn(eb, hhi)
            dva[win, :] += dot_tn(w, ghi)
            df = dot_nn(dkap, phk[0, win, :])
            if n:
                df = df + jnp.where(start < j0, dot_nt(ghi, states[n]), 0.0)
            dpq[rows, :] = df
            dpk[win, :] += dot_tn(dkap, phq[0, rows, :])
        back = None
        for n in reversed(range(T // CHUNK)):
            r0 = n * CHUNK
            j0 = max(r0 - BACK, 0)
            m = r0 + CHUNK - BACK - j0
            if back is not None:
                keys = pl.ds(j0, m)
                nstart = start_of(r0 + CHUNK, e0, e1)
                jc = j0 + lax.broadcasted_iota(jnp.int32, (m, 1), 0)
                bb = back.astype(BF)
                dpk[keys, :] += jnp.where(jc >= nstart, dot_nt(vaug[0, keys, :], bb), 0.0)
                dva[keys, :] += jnp.where(jc >= nstart, dot_nn(phk[0, keys, :], bb), 0.0)
                back = jnp.where(nstart < j0, back, 0.0)
            if n:
                rows = pl.ds(r0, CHUNK)
                start = start_col(r0, CHUNK, e0, e1)
                pq = jnp.where(start < j0, phq[0, rows, :].astype(F32), 0.0).astype(BF)
                add = dot_tn(pq, gvec[rows, :])
                back = add if back is None else back + add
        window = jnp.zeros((1, 128), F32)
        dmq = jnp.zeros((128, 128), F32)
        dmk = jnp.zeros((128, 128), F32)
        ones2 = jnp.concatenate([ones, ones], axis=0)
        for r0 in range(0, T, CHUNK):
            rows = pl.ds(r0, CHUNK)
            f = fq[rows, :]
            prod = f * (dpq[rows, :] * c)
            window = window + jnp.sum(prod, axis=0, keepdims=True)
            hi, lo = split2(prod)
            dp = (prod - f * dot_nn(jnp.concatenate([hi, lo], axis=1), ones2)).astype(BF)
            dmq = dmq + dot_tn(qaug[rows, 128:256], dp)
            dq = dqa[rows, :] * 0.125 + dot_nn(dp, mqt_ref[hh])
            dq = dq * cos_ref[rows, :] - spin(dq) * sin_ref[rows, :]
            keep = low if isinstance(hh, int) and hh == 0 else (low == (hh == 0))
            dq_ref[rows, :] = jnp.where(keep, dq, dq_ref[rows, :].astype(F32)).astype(BF)
            f = fk[rows, :]
            prod = f * dpk[rows, :]
            hi, lo = split2(prod)
            dp = (prod - f * dot_nn(jnp.concatenate([hi, lo], axis=1), ones2)).astype(BF)
            dmk = dmk + dot_tn(kaug[0, rows, 0:128], dp)
            dk_ref[rows, :] += dka[rows, :] * LN2 + dot_nn(dp, mkt_ref[hh])
            dv_ref[rows, :] += dva[rows, :]
        dmq = (dmq - swap(dmq)) * (8.0 * LN2)
        dmk = dmk - swap(dmk)
        gq_ref[hh] = dmq[0:64, 0:64]
        gk_ref[hh] = dmk[0:64, 0:64]
        st_ref[hh, 0:1, :] = square
        st_ref[hh, 1:2, :] = window
        return 0

    lax.fori_loop(0, 2, head, 0)

    for r0 in range(0, T, CHUNK):
        rows = pl.ds(r0, CHUNK)
        dk = dk_ref[rows, :]
        dk_ref[rows, :] = dk * cos_ref[rows, :] - spin(dk) * sin_ref[rows, :]


def rotary_tables(position):
    freq = 500000.0 ** (-2.0 * jnp.arange(32, dtype=F32) / 64)
    angle = position.astype(F32)[:, None] * freq[None, :]
    cosine, sine = jnp.cos(angle), jnp.sin(angle)
    return jnp.concatenate([cosine] * 4, axis=1), jnp.concatenate([-sine, sine] * 2, axis=1)


def pack_maps(maps, scale, keys):
    both = jnp.concatenate([maps, -maps], axis=2) * scale
    hi = lax.reduce_precision(both, 8, 7)
    lo = both - hi
    parts = [hi, lo, hi] if keys else [hi, hi, lo]
    return jnp.concatenate([*parts, jnp.zeros_like(lo)], axis=1).astype(BF)


def flip_maps(maps):
    both = jnp.swapaxes(jnp.concatenate([maps, -maps], axis=2), 1, 2)
    return jnp.concatenate([both, both], axis=2).astype(BF)


def attention_fwd(ends, cees, q, k, v, cosine, sine, mq, mk):
    T, H = q.shape[0], q.shape[1] // HD
    rep = 4
    full = lambda shape: pl.BlockSpec(shape, lambda p: (0,) * len(shape))
    pair = pl.BlockSpec((T, 128), lambda p: (0, p))
    heads = lambda *shape: pl.BlockSpec((2, *shape), lambda p: (p, 0, 0))
    smem = pl.BlockSpec(memory_space=pltpu.SMEM)
    return pl.pallas_call(
        functools.partial(fwd_kernel, rep=rep),
        grid=(H // 2,),
        in_specs=[smem, smem, pair, full((T, 128)), full((T, 128)), full((T, 128)), full((T, 128)),
                  heads(256, 128), heads(256, 128)],
        out_specs=[pair, heads(T, 128)],
        out_shape=[jax.ShapeDtypeStruct((T, H * HD), BF), jax.ShapeDtypeStruct((H, T, 128), F32)],
        scratch_shapes=[pltpu.VMEM((2, T, 256), BF), pltpu.VMEM((2, T, 128), BF), pltpu.VMEM((2, T, 256), BF),
                        pltpu.VMEM((2, T, 128), BF), pltpu.VMEM((2, T, 128), BF)],
        compiler_params=pltpu.CompilerParams(vmem_limit_bytes=48 * 2**20),
        cost_estimate=pl.CostEstimate(flops=H * 8 * 2**30, bytes_accessed=16 * 2**20, transcendentals=0),
        name="mix_forward",
    )(ends, cees, q, k, v, cosine, sine, mq, mk)


def attention_bwd(pair, ends, cees, q, k, v, cosine, sine, mq, mk, mqt, mkt, nm, da):
    T = q.shape[0]
    kv = 2 * pair // 4
    full = lambda shape: pl.BlockSpec(shape, lambda p: (0,) * len(shape))
    cols = pl.BlockSpec((T, 128), lambda p: (0, pair))
    heads = lambda *shape: pl.BlockSpec((2, *shape), lambda p: (pair, 0, 0))
    smem = pl.BlockSpec(memory_space=pltpu.SMEM)
    wide = full((T, 128))
    f32buf = pltpu.VMEM((T, 128), F32)
    return pl.pallas_call(
        functools.partial(bwd_kernel, pair=pair, kv=kv),
        grid=(1,),
        in_specs=[smem, smem, cols, wide, wide, wide, wide, heads(256, 128), heads(256, 128),
                  heads(128, 128), heads(128, 128), heads(T, 128), cols],
        out_specs=[wide, wide, wide, full((2, 64, 64)), full((2, 64, 64)), full((2, 8, 128))],
        out_shape=[jax.ShapeDtypeStruct((T, 128), BF), jax.ShapeDtypeStruct((T, 128), F32),
                   jax.ShapeDtypeStruct((T, 128), F32), jax.ShapeDtypeStruct((2, 64, 64), F32),
                   jax.ShapeDtypeStruct((2, 64, 64), F32), jax.ShapeDtypeStruct((2, 8, 128), F32)],
        scratch_shapes=[pltpu.VMEM((1, T, 256), BF), pltpu.VMEM((1, T, 128), BF),
                        pltpu.VMEM((T, 256), BF), f32buf, f32buf,
                        pltpu.VMEM((1, T, 128), BF), pltpu.VMEM((1, T, 128), BF),
                        pltpu.VMEM((T // CHUNK, 128, 128), BF), pltpu.VMEM((T, 128), BF),
                        f32buf, f32buf, f32buf, f32buf, f32buf],
        compiler_params=pltpu.CompilerParams(vmem_limit_bytes=56 * 2**20),
        cost_estimate=pl.CostEstimate(flops=30 * 10**9, bytes_accessed=8 * 2**20, transcendentals=0),
        name="mix_backward",
    )(ends, cees, q, k, v, cosine, sine, mq, mk, mqt, mkt, nm, da)


TILE = 256


def gated_kernel(x_ref, c_ref, wg_ref, wu_ref, wd_ref, *rest):
    act_ref, dg_ref, du_ref = rest[-3:]

    step = min(768, x_ref.shape[0])

    def some(n, _):
        rows = pl.ds(pl.multiple_of(n * step, step), step)
        x = x_ref[rows, :]
        gate = dot_nn(x, wg_ref[...])
        up = dot_nn(x, wu_ref[...])
        da = dot_nt(c_ref[rows, :], wd_ref[...])
        s = 1.0 / (1.0 + jnp.exp(-gate))
        gs = gate * s
        act_ref[rows, :] = (gs * up).astype(BF)
        du_ref[rows, :] = (da * gs).astype(BF)
        dg_ref[rows, :] = (da * up * (s + gs * (1.0 - s))).astype(BF)
        return 0

    lax.fori_loop(0, x_ref.shape[0] // step, some, 0)


def gated(x, cot, wg, wu, wd, part, parts, rows, row_block, group_rows, act, dg, du):
    width = x.shape[1]
    hidden = wg.shape[1] // parts
    tiles = hidden // TILE
    first = part * tiles
    blocks = x.shape[0] // rows
    left = pl.BlockSpec((rows, width), lambda n, r: (r, 0))
    column = pl.BlockSpec((width, TILE), lambda n, r: (0, first + n))
    tile = pl.BlockSpec((rows, TILE), lambda n, r: (row_block + r, n))
    wide = pl.BlockSpec((rows, TILE), lambda n, r: (row_block + r, first + n))
    specs = [left, left, column, column, pl.BlockSpec((TILE, width), lambda n, r: (first + n, 0))]
    args = [x, cot, wg, wu, wd]
    aliases = {}
    for k, value in enumerate((act, dg, du)):
        if value is not None:
            aliases[len(args)] = k
            args.append(value)
            specs.append(pl.BlockSpec(memory_space=pl.ANY))
    return pl.pallas_call(
        gated_kernel,
        grid=(tiles, blocks),
        in_specs=specs,
        out_specs=[tile, wide, wide],
        out_shape=[
            jax.ShapeDtypeStruct((group_rows, hidden), BF),
            jax.ShapeDtypeStruct((group_rows, hidden * parts), BF),
            jax.ShapeDtypeStruct((group_rows, hidden * parts), BF),
        ],
        input_output_aliases=aliases,
        compiler_params=pltpu.CompilerParams(vmem_limit_bytes=48 * 2**20),
        cost_estimate=pl.CostEstimate(
            flops=6 * x.shape[0] * width * hidden,
            bytes_accessed=4 * x.shape[0] * width + 6 * width * hidden,
            transcendentals=0,
        ),
        name="gated",
    )(*args)


ASKER_COUNT = 32
norm_eps = 1e-05
factored_multiplier = 2.0


def plain_contract(left, right):
    return jnp.dot(left, right, preferred_element_type=jnp.float32)


def transposed_right_product(left, right):
    return dot_nt(left, right)


def flipped_first_contract(left, right):
    return dot_tn(left, right)


def after(value, *done):
    return lax.optimization_barrier((value, *done))[0]


class Swaps:
    def __init__(self, axis):
        self.axis = axis
        self.count = lax.axis_size(axis)
        self.bits = self.count.bit_length() - 1
        self.me = lax.axis_index(axis)
        self.last = None

    def bit(self, b):
        return self.me // (1 << b) % 2

    def swap(self, value, b):
        return lax.ppermute(value, self.axis, [(i, i ^ (1 << b)) for i in range(self.count)])

    def queued(self, value, b):
        if self.last is not None:
            value = after(value, self.last)
        self.last = self.swap(value, b)
        return self.last


def row_order(mp):
    far = [0]
    for b in reversed(range(1, mp.bits)):
        far = far + [r ^ (1 << b) for r in far]
    far = far[1:]
    return [0, 1] + far + [r ^ 1 for r in far]


def gather_far(value, mp):
    rows = value.shape[0]
    for b in reversed(range(1, mp.bits)):
        got = mp.swap(value, b)
        value = got if mp.bits == 2 else jnp.concatenate([value, got], axis=0)
    return value if mp.bits == 2 else value[rows:]


def with_partner(value, mp):
    return jnp.concatenate([value, mp.swap(value, 0)], axis=0)


def scatter_rows(near, far, mp):
    half = far.shape[0] // 2
    got = mp.swap(far[half:], 0)
    far = (far[:half].astype(F32) + got.astype(F32)).astype(BF)
    rows = near.shape[0] // 2
    order = row_order(mp)[2 : 2 + half // rows]
    blocks = {r: far[k * rows : (k + 1) * rows] for k, r in enumerate(order)}
    got = mp.swap(near[rows:], 0)
    blocks[0] = near[:rows].astype(F32) + got.astype(F32)
    for b in reversed(range(1, mp.bits)):
        sent = [r for r in sorted(blocks) if r >> b & 1]
        send = [blocks.pop(r) for r in sent]
        got = mp.swap(send[0] if len(send) == 1 else jnp.concatenate(send, axis=0).astype(BF), b)
        for k, r in enumerate(sent):
            to = r ^ (1 << b)
            blocks[to] = blocks[to].astype(F32) + got[k * rows : (k + 1) * rows].astype(F32)
            if to:
                blocks[to] = blocks[to].astype(BF)
    return blocks[0]


def to_order(value, mp):
    order = row_order(mp)
    inverse = jnp.asarray([order.index(r) for r in range(mp.count)], jnp.int32)
    rows = value.shape[0] // mp.count
    blocks = [
        lax.dynamic_slice_in_dim(
            value, lax.dynamic_index_in_dim(inverse, a ^ mp.me, keepdims=False) * rows, rows, 0
        )
        for a in range(mp.count)
    ]
    return jnp.concatenate(blocks, axis=0)


def from_order(value, mp):
    rows = value.shape[0] // mp.count
    return [lax.dynamic_slice_in_dim(value, (mp.me ^ r) * rows, rows, 0) for r in row_order(mp)]


def take_half(value, index):
    half = value.shape[0] // 2
    return lax.dynamic_slice_in_dim(value, index * half, half, 0)


def place_kernel(at_ref, mine_ref, got_ref, *rest):
    first = pl.program_id(0) < pl.num_programs(0) // 2
    rest[-1][...] = jnp.where(first, mine_ref[...].astype(F32), got_ref[...].astype(F32))


def place(mine, got, at, into, part, parts):
    count = at.shape[0]
    rows, cols = mine.shape[0] * 2 // count, mine.shape[1]
    half = count // 2
    specs = [
        pl.BlockSpec((rows, cols), lambda r, at: (jnp.minimum(r, half - 1), 0)),
        pl.BlockSpec((rows, cols), lambda r, at: (jnp.maximum(r - half, 0), 0)),
    ]
    args = [at + part * count, mine, got]
    if into is not None:
        specs.append(pl.BlockSpec(memory_space=pl.ANY))
        args.append(into)
    return pl.pallas_call(
        place_kernel,
        grid_spec=pltpu.PrefetchScalarGridSpec(
            num_scalar_prefetch=1,
            grid=(count,),
            in_specs=specs,
            out_specs=pl.BlockSpec((rows, cols), lambda r, at: (at[r], 0)),
        ),
        out_shape=jax.ShapeDtypeStruct((mine.shape[0] * 2 * parts, cols), F32),
        input_output_aliases={} if into is None else {3: 0},
        compiler_params=pltpu.CompilerParams(vmem_limit_bytes=24 * 2**20),
        cost_estimate=pl.CostEstimate(
            flops=0, bytes_accessed=mine.shape[0] * cols * 12, transcendentals=0
        ),
        name="place",
    )(*args)


class Sum:
    def __init__(self, lane, part, at=0, parts=1):
        self.lane, self.at, self.parts = lane, at, parts
        for b in range(lane.bits):
            if b:
                part = (self.keep.astype(F32) + self.got.astype(F32)).astype(BF)
            self.keep = take_half(part, lane.bit(b))
            self.got = lane.queued(take_half(part, 1 - lane.bit(b)), b)

    def scatter(self, after=None):
        got = self.got
        if after is not None:
            got = lax.optimization_barrier((got, *(after if isinstance(after, tuple) else (after,))))[0]
        part = (self.keep.astype(F32) + got.astype(F32)).astype(BF)
        self.seen = part
        self.part = lax.psum_scatter(part, "z", scatter_dimension=0, tiled=True)
        self.value = lax.all_gather(self.part, "z", axis=0, tiled=True)

    def gather(self):
        lane = self.lane
        for b in reversed(range(lane.bits)):
            self.got = lane.queued(self.value, b)
            if b:
                self.value = jnp.concatenate([self.value, self.got], axis=0)

    def finish(self, into):
        lane = self.lane
        sub = 4
        steps = jnp.arange(lane.count * sub, dtype=jnp.int32)
        at = steps % sub
        for k, b in enumerate(reversed(range(lane.bits))):
            at = at + ((steps // sub // (1 << k) % 2) ^ lane.bit(b)) * (sub << k)
        return place(self.value, self.got, at, into, self.at, self.parts)


def pad_rows(value, rows):
    return jnp.pad(value, ((0, rows - value.shape[0]), (0, 0)))


def round_up(value, unit):
    return -(-value // unit) * unit


def rms_scale(values):
    return lax.rsqrt(jnp.mean(values * values, axis=-1, keepdims=True) + norm_eps)


def norm_back(values, scale_in, gain_in, grad_normed):
    weighted = grad_normed * gain_in
    grad_values = scale_in * weighted - values * (scale_in * scale_in * scale_in) * jnp.mean(
        weighted * values, axis=-1, keepdims=True
    )
    grad_gain = jnp.sum(grad_normed * values * scale_in, axis=0)
    return (grad_values, grad_gain)


def local(
    layer_tokens,
    sequence_extents,
    loss_sensitivity,
    mixing_rms_gain,
    asker_dense_map,
    lookup_dense_map,
    content_dense_map,
    shrink_map_asker,
    grow_map_asker,
    shrink_map_lookup,
    grow_map_lookup,
    shrink_map_content,
    grow_map_content,
    asker_feature_maps,
    lookup_feature_maps,
    local_portion_logit,
    emitted_mixing_map,
    emitted_shrink_map,
    emitted_grow_map,
    feedforward_rms_gain,
    gating_dense_map,
    widen_dense_map,
    shrink_dense_map,
):
    rows_dev = layer_tokens.shape[0]
    width = layer_tokens.shape[1]
    mp, lane = Swaps("mp"), Swaps("x")
    unit = 16 * lane.count * lax.axis_size("z")
    group_rows = rows_dev * lax.axis_size("mp")
    tokens_all = group_rows * lax.axis_size("z") * lax.axis_size("x")
    heads_dev = asker_dense_map.shape[1] // HD
    key_heads = lookup_dense_map.shape[1] // HD
    rank_width = shrink_map_asker.shape[1]
    first_end = sequence_extents[0, 0]
    second_end = first_end + sequence_extents[0, 1]
    ends = jnp.stack([first_end, second_end])
    places = jnp.arange(group_rows, dtype=jnp.int32)
    position = places - start_of(places, first_end, second_end)
    cosine, sine = rotary_tables(position)
    residual_in = layer_tokens.astype(jnp.float32)
    scale_one = rms_scale(residual_in)
    normalized_input = (residual_in * scale_one * mixing_rms_gain).astype(jnp.bfloat16)
    q_cols, k_cols = heads_dev * HD, key_heads * HD
    near_rows = 2 * rows_dev
    normed_near = with_partner(normalized_input, mp)
    normed_far = gather_far(normalized_input, mp)
    dense_all = jnp.concatenate(
        [asker_dense_map, lookup_dense_map, content_dense_map], axis=1
    )
    a_all_wide = jnp.concatenate([shrink_map_asker, shrink_map_lookup, shrink_map_content], axis=1)
    grow_all = jnp.concatenate(
        [
            jnp.pad(grow_map_asker, ((0, 0), (0, 2 * k_cols))),
            jnp.pad(grow_map_lookup, ((0, 0), (q_cols, k_cols))),
            jnp.pad(grow_map_content, ((0, 0), (q_cols + k_cols, 0))),
        ],
        axis=0,
    )
    dense_all = (
        dense_all.astype(F32) + factored_multiplier * plain_contract(a_all_wide, grow_all)
    ).astype(BF)
    mixing_map = (
        emitted_mixing_map.astype(F32)
        + factored_multiplier * plain_contract(emitted_shrink_map, emitted_grow_map)
    ).astype(BF)
    cees = jnp.exp(-local_portion_logit)
    tables = (
        pack_maps(asker_feature_maps, 8.0, False),
        pack_maps(lookup_feature_maps, LOG2E, True),
    )
    flipped = (flip_maps(asker_feature_maps), flip_maps(lookup_feature_maps))
    projected_near = plain_contract(normed_near, dense_all).astype(BF)
    normed_far = after(
        normed_far, dense_all, mixing_map, cees, cosine, sine, *tables, *flipped, projected_near
    )
    loss_far = gather_far(after(loss_sensitivity, normed_far), mp)
    normed_far = with_partner(normed_far, mp)
    projected_far = plain_contract(normed_far, dense_all).astype(BF)
    projected = to_order(jnp.concatenate([projected_near, projected_far], axis=0), mp)
    spare = max(0, 128 - k_cols)
    key_proj = jnp.pad(projected[:, q_cols : q_cols + k_cols], ((0, 0), (0, spare)))
    value_proj = jnp.pad(projected[:, q_cols + k_cols :], ((0, 0), (0, spare)))
    attention_args = (
        ends, cees, projected[:, :q_cols], key_proj, value_proj, cosine, sine, *tables
    )
    mixing_outcome, mixed_kept = attention_fwd(*attention_args)
    mixing_outcome, loss_far = lax.optimization_barrier((mixing_outcome, loss_far))
    mixing_blocks = from_order(mixing_outcome, mp)
    mixing_far = jnp.concatenate(mixing_blocks[2:], axis=0)
    mixing_near = jnp.concatenate(mixing_blocks[:2], axis=0)
    branch_far = plain_contract(mixing_far, mixing_map).astype(BF)
    branch_near = plain_contract(after(mixing_near, branch_far), mixing_map).astype(BF)
    hidden = residual_in + scatter_rows(branch_near, branch_far, mp)
    cot_later = after(loss_sensitivity, branch_near)
    cot_near = with_partner(cot_later, mp)
    cot_far = with_partner(loss_far, mp)
    cot_rows = jnp.concatenate([cot_near, cot_far], axis=0)
    hidden = after(hidden, cot_rows)
    scale_two = rms_scale(hidden)
    normed_two = (hidden * scale_two * feedforward_rms_gain).astype(BF)
    gathered_near = with_partner(normed_two, mp)
    gathered_far = gather_far(normed_two, mp)
    halves = 2
    acts = [None, None]
    d_gate = d_up = None
    for n in range(halves):
        acts[n], d_gate, d_up = gated(
            gathered_near, cot_near, gating_dense_map, widen_dense_map, shrink_dense_map,
            n, halves, near_rows, 0, group_rows, None, d_gate, d_up,
        )
    gathered_far = with_partner(after(gathered_far, d_gate), mp)
    downs = []
    for n in range(halves):
        acts[n], d_gate, d_up = gated(
            gathered_far, cot_far, gating_dense_map, widen_dense_map, shrink_dense_map,
            n, halves, near_rows, 1, group_rows, acts[n], d_gate, d_up,
        )
        downs.append(flipped_first_contract(acts[n], cot_rows).astype(BF))
        if n == 0:
            gathered_far = after(gathered_far, downs[0])
    down_one = Sum(lane, downs[0], parts=2)
    through_gate = transposed_right_product(after(d_gate, downs[1]), gating_dense_map)
    down_one.scatter(after=through_gate)
    down_two = Sum(lane, downs[1], at=1, parts=2)
    d_normed_part = (
        through_gate + transposed_right_product(after(d_up, down_one.seen), widen_dense_map)
    ).astype(BF)
    gathered_two = jnp.concatenate([gathered_near, gathered_far], axis=0)
    collected_rows = jnp.concatenate([normed_near, normed_far], axis=0)
    mixing_outcome = jnp.concatenate([mixing_near, mixing_far], axis=0)
    middle_rows = plain_contract(after(collected_rows, d_normed_part), a_all_wide).astype(BF)
    emitted_inner_tokens = plain_contract(
        after(mixing_outcome, d_normed_part), emitted_shrink_map
    ).astype(BF)
    d_normed_two = scatter_rows(d_normed_part[:near_rows], d_normed_part[near_rows:], mp)
    gate_part = flipped_first_contract(after(gathered_two, d_normed_part), d_gate).astype(BF)
    down_two.scatter(after=gate_part)
    gate_sum = Sum(lane, gate_part)
    up_part = flipped_first_contract(after(gathered_two, down_two.seen), d_up).astype(BF)
    d_normed_two = after(d_normed_two, up_part)
    d_hidden_norm, grad_norm_two = norm_back(hidden, scale_two, feedforward_rms_gain, d_normed_two)
    d_hidden = loss_sensitivity.astype(F32) + d_hidden_norm
    d_branch = d_hidden.astype(BF)
    d_branch_near = with_partner(d_branch, mp)
    d_branch_far = with_partner(gather_far(d_branch, mp), mp)
    factored_path_derivative = jnp.concatenate([d_branch_near, d_branch_far], axis=0)
    d_attended = to_order(transposed_right_product(factored_path_derivative, mixing_map), mp)
    d_attended = after(d_attended, down_one.value)
    gate_sum.scatter(after=d_attended)
    d_attended = after(d_attended, gate_sum.seen)
    up_sum = Sum(lane, up_part)
    pairs = heads_dev // 2
    pair_outs = []
    for n in range(pairs):
        pair_outs.append(attention_bwd(n, *attention_args, *flipped, mixed_kept, d_attended))
        done = pair_outs[-1][0]
        d_attended = after(d_attended, done)
        if n == 0:
            d_attended = after(d_attended, down_two.value)
        if n == pairs - 2:
            up_sum.scatter(after=done)
            d_attended = after(d_attended, up_sum.seen)
            down_one.gather()
    emitted_inner_derivative = (
        factored_multiplier * transposed_right_product(factored_path_derivative, emitted_grow_map)
    ).astype(BF)
    per_kv = pairs // key_heads
    d_keys, d_values = (
        jnp.concatenate(
            [
                sum(pair_outs[kv * per_kv + n][which][:, :HD] for n in range(per_kv))
                for kv in range(key_heads)
            ],
            axis=1,
        ).astype(BF)
        for which in (1, 2)
    )
    projected_gradient = jnp.concatenate(
        from_order(
            jnp.concatenate([outs[0] for outs in pair_outs] + [d_keys, d_values], axis=1), mp
        ),
        axis=0,
    )
    grad_query_maps = jnp.concatenate([outs[3] for outs in pair_outs], axis=0)
    grad_key_maps = jnp.concatenate([outs[4] for outs in pair_outs], axis=0)
    kept_sums = jnp.concatenate([outs[5] for outs in pair_outs], axis=0)
    combined_middle_gradient = (
        factored_multiplier * transposed_right_product(projected_gradient, grow_all)
    ).astype(BF)
    d_normed_part = transposed_right_product(projected_gradient, dense_all).astype(BF)
    d_normed = scatter_rows(d_normed_part[:near_rows], d_normed_part[near_rows:], mp)
    left = after(projected_gradient, d_normed_part)
    grad_w_all = flipped_first_contract(collected_rows, left)
    grow = factored_multiplier * flipped_first_contract(middle_rows, left)
    both = jnp.concatenate([grad_w_all.astype(BF), grow.astype(BF)], axis=0)
    proj_sum = Sum(lane, pad_rows(both, round_up(both.shape[0], unit)))
    half = shrink_dense_map.shape[0] // 2
    mlp_part = (
        plain_contract(after(acts[0], left), shrink_dense_map[:half])
        + plain_contract(acts[1], shrink_dense_map[half:])
    ).astype(BF)
    mlp_part = after(mlp_part, d_normed)
    output = (hidden + scatter_rows(mlp_part[:near_rows], mlp_part[near_rows:], mp)).astype(BF)
    grad_w_out = flipped_first_contract(mixing_outcome, factored_path_derivative).astype(BF)
    d_inputs_norm, grad_norm_one = norm_back(residual_in, scale_one, mixing_rms_gain, d_normed)
    input_grad = (d_hidden + d_inputs_norm).astype(BF)
    grad_a_all = flipped_first_contract(collected_rows, combined_middle_gradient)
    grad_a_out = flipped_first_contract(mixing_outcome, emitted_inner_derivative)
    emitted_grow_derivative = factored_multiplier * flipped_first_contract(
        emitted_inner_tokens, factored_path_derivative
    )
    shared = jnp.concatenate(
        [
            grad_norm_one[None],
            grad_norm_two[None],
            grad_a_all.T,
            emitted_grow_derivative,
            jnp.pad(jnp.sum(kept_sums[:, 0, :HD], axis=0), (0, width - HD))[None],
        ],
        axis=0,
    )

    for b in range(mp.bits):
        shared = shared + mp.swap(shared, b)
    n_shared = shared.shape[0]
    window_lanes = -kept_sums[:, 1, :]
    own = [grad_a_out, grad_query_maps, grad_key_maps, window_lanes]
    flat = jnp.concatenate([value.reshape(-1) for value in own])
    flat = jnp.pad(flat, (0, round_up(flat.shape[0], width) - flat.shape[0])).reshape(-1, width)
    last = jnp.concatenate([grad_w_out, shared.astype(BF), flat.astype(BF)], axis=0)
    proj_sum.scatter()
    out_sum = Sum(lane, pad_rows(last, round_up(last.shape[0], unit)))
    out_sum.scatter()
    for item in (down_two, gate_sum, up_sum):
        item.gather()
    grad_w_down = down_two.finish(down_one.finish(None))
    proj_sum.value = after(proj_sum.value, grad_w_down)
    proj_sum.gather()
    grad_w_gate = gate_sum.finish(None)
    out_sum.value = after(out_sum.value, grad_w_gate)
    out_sum.gather()
    grad_w_up, total, last_total = (item.finish(None) for item in (up_sum, proj_sum, out_sum))
    grad_w_query = total[:width, :q_cols]
    grad_w_key = total[:width, q_cols : q_cols + k_cols]
    grad_w_value = total[:width, q_cols + k_cols :]
    grow = total[width : width + 3 * rank_width]
    asker_grow_derivative = grow[:rank_width, :q_cols]
    lookup_grow_derivative = grow[rank_width : 2 * rank_width, q_cols : q_cols + k_cols]
    content_grow_derivative = grow[2 * rank_width : 3 * rank_width, q_cols + k_cols :]
    total = last_total
    out_rows = grad_w_out.shape[0]
    grad_w_out = total[:out_rows]
    shared = total[out_rows : out_rows + n_shared]
    grad_norm_one, grad_norm_two = shared[0], shared[1]
    grad_a_all = shared[2 : 2 + 3 * rank_width].T
    grad_a_query = grad_a_all[:, :rank_width]
    grad_a_key = grad_a_all[:, rank_width : 2 * rank_width]
    grad_a_value = grad_a_all[:, 2 * rank_width :]
    emitted_grow_derivative = shared[2 + 3 * rank_width : n_shared - 1]
    teacher_sq = jnp.sum(shared[n_shared - 1, :HD])
    flat = total[out_rows + n_shared :].reshape(-1)
    split = []
    for value in own:
        split.append(flat[: value.size].reshape(value.shape))
        flat = flat[value.size :]
    grad_a_out, grad_query_maps, grad_key_maps, window_lanes = split
    grad_window = jnp.sum(window_lanes, axis=1)
    teacher_mse = teacher_sq / float(tokens_all * ASKER_COUNT * HD)
    return (
        output,
        input_grad,
        grad_norm_one,
        grad_w_query,
        grad_w_key,
        grad_w_value,
        grad_a_query,
        asker_grow_derivative,
        grad_a_key,
        lookup_grow_derivative,
        grad_a_value,
        content_grow_derivative,
        grad_query_maps,
        grad_key_maps,
        grad_window,
        grad_w_out,
        grad_a_out,
        emitted_grow_derivative,
        grad_norm_two,
        grad_w_gate,
        grad_w_up,
        grad_w_down,
        teacher_mse,
    )


def solution(mesh):
    split = jax.sharding.Mesh(
        mesh.devices.reshape(4, mesh.shape["batch"] // 4, mesh.shape["mp"]), ("z", "x", "mp")
    )
    return jax.shard_map(
        local,
        mesh=split,
        in_specs=(
            P(("z", "x", "mp"), None),
            P(("z", "x"), None),
            P(("z", "x", "mp"), None),
            P(),
            P(None, "mp"),
            P(None, "mp"),
            P(None, "mp"),
            P(),
            P(None, "mp"),
            P(),
            P(None, "mp"),
            P(),
            P(None, "mp"),
            P("mp", None, None),
            P("mp", None, None),
            P("mp"),
            P("mp", None),
            P("mp", None),
            P(),
            P(),
            P(None, "mp"),
            P(None, "mp"),
            P("mp", None),
        ),
        out_specs=(
            P(("z", "x", "mp"), None),
            P(("z", "x", "mp"), None),
            P(),
            P(None, "mp"),
            P(None, "mp"),
            P(None, "mp"),
            P(),
            P(None, "mp"),
            P(),
            P(None, "mp"),
            P(),
            P(None, "mp"),
            P("mp", None, None),
            P("mp", None, None),
            P("mp"),
            P("mp", None),
            P("mp", None),
            P(),
            P(),
            P(None, "mp"),
            P(None, "mp"),
            P("mp", None),
            P(),
        ),
        check_vma=False,
    )
```

```python
import functools
import math
import jax
import jax.numpy as jnp
from jax import lax
from jax.experimental import pallas as pl
from jax.experimental.pallas import tpu as pltpu
from jax.sharding import PartitionSpec as P

HD = 64
WINDOW = 64
CHUNK = 256
BACK = 128
LOG2E = math.log2(math.e)
LN2 = math.log(2.0)
BIG = 16384.0
F32 = jnp.float32
BF = jnp.bfloat16


def dot_nn(a, b):
    return lax.dot_general(a, b, (((1,), (0,)), ((), ())), preferred_element_type=F32)


def dot_nt(a, b):
    return lax.dot_general(a, b, (((1,), (1,)), ((), ())), preferred_element_type=F32)


def dot_tn(a, b):
    return lax.dot_general(a, b, (((0,), (0,)), ((), ())), preferred_element_type=F32)


def lanes(rows):
    return lax.broadcasted_iota(jnp.int32, (rows, 128), 1)


def swap(x):
    return pltpu.roll(x, 64, 1)


def spin(x):
    lane = lanes(x.shape[0])
    return jnp.where((lane & 63) < 32, pltpu.roll(x, 96, 1), pltpu.roll(x, 32, 1))


def twin(x, odd):
    low = lanes(x.shape[0]) < 64
    other = swap(x)
    return jnp.where(low != odd, x, other)


def half_ones():
    r = lax.broadcasted_iota(jnp.int32, (128, 128), 0)
    c = lax.broadcasted_iota(jnp.int32, (128, 128), 1)
    return ((r < 64) == (c < 64)).astype(BF)


def start_of(t, e0, e1):
    return jnp.where(t >= e1, e1, jnp.where(t >= e0, e0, 0))


def start_col(r0, rows, e0, e1):
    t = r0 + lax.broadcasted_iota(jnp.int32, (rows, 1), 0)
    return start_of(t, e0, e1)


def prep_keys(k_ref, v_ref, cos_ref, sin_ref, kaug, vaug, seg, e0, e1, heads=(0, 1)):
    T = k_ref.shape[0]
    for r0 in range(0, T, CHUNK):
        rows = pl.ds(r0, CHUNK)
        k = k_ref[rows, :].astype(F32)
        v = v_ref[rows, :].astype(F32)
        kr = k * cos_ref[rows, :] + spin(k) * sin_ref[rows, :]
        lane = lanes(CHUNK)
        low = lane < 64
        if seg:
            t = r0 + lax.broadcasted_iota(jnp.int32, (CHUNK, 1), 0)
            mine = (t >= e0).astype(jnp.int32) + (t >= e1).astype(jnp.int32) + 64
            tail = jnp.where((lane < 67) & (lane != mine), -BIG, 0.0)
        else:
            tail = 0.0
        for at, kv in enumerate(heads):
            x = twin(kr, kv == 1)
            hi = x.astype(BF)
            lo = x - hi.astype(F32)
            kaug[at, rows, 0:128] = hi
            kaug[at, rows, 128:256] = jnp.where(low, lo, tail).astype(BF)
            vaug[at, rows, :] = jnp.where(low, v if kv == 0 else swap(v), 1.0).astype(BF)


def prep_query(qr, odd, seg, r0, e0, e1):
    x = twin(qr, odd)
    hi = x.astype(BF)
    lo = (x - hi.astype(F32)).astype(BF)
    lane = lanes(x.shape[0])
    low = lane < 64
    first = jnp.where(low, hi, lo)
    second = hi
    if seg:
        t = r0 + lax.broadcasted_iota(jnp.int32, (x.shape[0], 1), 0)
        mine = (t >= e0).astype(jnp.int32) + (t >= e1).astype(jnp.int32) + 64
        second = jnp.where(low, hi.astype(F32), jnp.where(lane == mine, 1.0, 0.0)).astype(BF)
    return first, second


def features(aug, maps, ones):
    p = jnp.exp2(dot_nn(aug, maps))
    return p / dot_nn(p.astype(BF), ones)


def fwd_kernel(e_ref, c_ref, q_ref, k_ref, v_ref, cos_ref, sin_ref, mq_ref, mk_ref,
               att_ref, nm_ref, kaug, vaug, qaug, phq, phk, *, rep):
    T = q_ref.shape[0]
    e0, e1 = e_ref[0], e_ref[1]
    p = pl.program_id(0)

    @pl.when(p == 0)
    def _():
        prep_keys(k_ref, v_ref, cos_ref, sin_ref, kaug, vaug, False, e0, e1)

    kv = (2 * p) // rep
    ones = half_ones()
    low = lanes(CHUNK) < 64
    for r0 in range(0, T, CHUNK):
        rows = pl.ds(r0, CHUNK)
        q = q_ref[rows, :].astype(F32) * (LOG2E / 8.0)
        qr = q * cos_ref[rows, :] + spin(q) * sin_ref[rows, :]
        for hh in range(2):
            first, second = prep_query(qr, hh == 1, False, r0, e0, e1)
            qaug[hh, rows, 0:128] = first
            qaug[hh, rows, 128:256] = second
            c = c_ref[2 * p + hh]
            phq[hh, rows, :] = (features(qaug[hh, rows, :], mq_ref[hh], ones) * c).astype(BF)
            phk[hh, rows, :] = features(kaug[kv, rows, :], mk_ref[hh], ones).astype(BF)
    for hh in range(2):
        state = None
        for r0 in range(0, T, CHUNK):
            rows = pl.ds(r0, CHUNK)
            j0 = max(r0 - BACK, 0)
            J = r0 + CHUNK - j0
            win = pl.ds(j0, J)
            ee = jnp.exp2(dot_nt(qaug[hh, rows, :], kaug[kv, win, :]))
            kap = dot_nt(phq[hh, rows, :], phk[hh, win, :])
            tt = r0 + lax.broadcasted_iota(jnp.int32, (CHUNK, J), 0)
            jj = j0 + lax.broadcasted_iota(jnp.int32, (CHUNK, J), 1)
            start = start_col(r0, CHUNK, e0, e1)
            w = jnp.where(tt - jj >= WINDOW, kap, ee)
            w = jnp.where((tt >= jj) & (jj >= start), w, 0.0)
            nd = dot_nn(w.astype(BF), vaug[kv, win, :])
            if state is not None:
                far = dot_nn(phq[hh, rows, :], state.astype(BF))
                nd = nd + jnp.where(start < j0, far, 0.0)
            rec = 1.0 / nd
            mix = nd * swap(rec)
            nm_ref[hh, rows, :] = jnp.where(low, mix, rec)
            if hh == 0:
                att_ref[rows, :] = mix.astype(BF)
            else:
                att_ref[rows, :] = jnp.where(low, att_ref[rows, :].astype(F32), swap(mix)).astype(BF)
            if r0 + CHUNK < T:
                state = next_state(state, phk, vaug, hh, kv, r0, j0, e0, e1)


def next_state(state, phk, vaug, hh, kv, r0, j0, e0, e1):
    n = r0 + CHUNK - BACK - j0
    nstart = start_of(r0 + CHUNK, e0, e1)
    jc = j0 + lax.broadcasted_iota(jnp.int32, (n, 1), 0)
    new = jnp.where(jc >= nstart, phk[hh, pl.ds(j0, n), :].astype(F32), 0.0).astype(BF)
    add = dot_tn(new, vaug[kv, pl.ds(j0, n), :])
    if state is None:
        return add
    return jnp.where(nstart < j0, state, 0.0) + add


def split2(x):
    hi = x.astype(BF)
    return hi, (x - hi.astype(F32)).astype(BF)


def bwd_kernel(e_ref, c_ref, q_ref, k_ref, v_ref, cos_ref, sin_ref, mq_ref, mk_ref, mqt_ref, mkt_ref,
               nm_ref, da_ref, dq_ref, dk_ref, dv_ref, gq_ref, gk_ref, st_ref,
               kaug, vaug, qaug, fq, fk, phq, phk, states, gvec, dpq, dpk, dqa, dva, dka, *, pair, kv):
    T = q_ref.shape[0]
    e0, e1 = e_ref[0], e_ref[1]
    prep_keys(k_ref, v_ref, cos_ref, sin_ref, kaug, vaug, True, e0, e1, (kv,))
    dk_ref[...] = jnp.zeros_like(dk_ref)
    dv_ref[...] = jnp.zeros_like(dv_ref)
    ones = half_ones()
    low = lanes(CHUNK) < 64
    lane = lanes(CHUNK)

    def head(hh, _):
        odd = hh == 1
        c = c_ref[2 * pair + hh]
        state = None
        for n, r0 in enumerate(range(0, T, CHUNK)):
            rows = pl.ds(r0, CHUNK)
            q = q_ref[rows, :].astype(F32) * (LOG2E / 8.0)
            qr = q * cos_ref[rows, :] + spin(q) * sin_ref[rows, :]
            first, second = prep_query(qr, odd, True, r0, e0, e1)
            qaug[rows, 0:128] = first
            qaug[rows, 128:256] = second
            f = features(qaug[rows, :], mq_ref[hh], ones)
            fq[rows, :] = f
            phq[0, rows, :] = (f * c).astype(BF)
            f = features(kaug[0, rows, :], mk_ref[hh], ones)
            fk[rows, :] = f
            phk[0, rows, :] = f.astype(BF)
            j0 = max(r0 - BACK, 0)
            if state is not None:
                states[n] = state.astype(BF)
            if r0 + CHUNK < T:
                state = next_state(state, phk, vaug, 0, 0, r0, j0, e0, e1)
        dpk[...] = jnp.zeros_like(dpk)
        dva[...] = jnp.zeros_like(dva)
        dka[...] = jnp.zeros_like(dka)
        square = jnp.zeros((1, 128), F32)
        for n, r0 in enumerate(range(0, T, CHUNK)):
            rows = pl.ds(r0, CHUNK)
            wide = pl.ds(0, r0 + CHUNK)
            diag = pl.ds(r0, CHUNK)
            tcol = r0 + lax.broadcasted_iota(jnp.int32, (CHUNK, 1), 0)
            start = start_of(tcol, e0, e1)
            full = r0 + CHUNK
            s = dot_nt(qaug[rows, :], kaug[0, wide, :])
            tt = r0 + lax.broadcasted_iota(jnp.int32, (CHUNK, full), 0)
            jj = lax.broadcasted_iota(jnp.int32, (CHUNK, full), 1)
            ee = jnp.exp2(s)
            ee = jnp.where(tt >= jj, ee, 0.0)
            eb = ee.astype(BF)
            nd = dot_nn(eb, vaug[0, wide, :])
            rec = 1.0 / nd
            soft = nd * swap(rec)
            soft = jnp.where(low, soft, swap(soft))
            srec = jnp.where(low, swap(rec), rec)
            nm = nm_ref[hh, rows, :]
            other = swap(nm)
            mix = jnp.where(low, nm, other)
            mrec = jnp.where(low, other, nm)
            delta = jnp.where(tcol < e1, mix - soft, 0.0)
            square = square + jnp.sum(delta * delta, axis=0, keepdims=True)
            g = twin(da_ref[rows, :], odd) + delta
            gd = -0.5 * jnp.sum(g * mix, axis=1, keepdims=True)
            gx = jnp.where(low, g, jnp.where(lane == 64, gd, 0.0)) * mrec
            hd = 0.5 * jnp.sum(delta * soft, axis=1, keepdims=True)
            hx = jnp.where(low, -delta, jnp.where(lane == 64, hd, 0.0)) * srec
            ghi, glo = split2(gx)
            hhi, hlo = split2(hx)
            gvec[rows, :] = ghi
            va = vaug[0, wide, :]
            r = dot_nt(jnp.concatenate([hhi, hlo], axis=1), jnp.concatenate([va, va], axis=1))
            j0 = max(r0 - BACK, 0)
            J = full - j0
            win = pl.ds(j0, J)
            vw = vaug[0, win, :]
            pw = dot_nt(jnp.concatenate([ghi, glo], axis=1), jnp.concatenate([vw, vw], axis=1))
            kap = dot_nt(phq[0, rows, :], phk[0, win, :])
            tw = r0 + lax.broadcasted_iota(jnp.int32, (CHUNK, J), 0)
            jw = j0 + lax.broadcasted_iota(jnp.int32, (CHUNK, J), 1)
            far = tw - jw >= WINDOW
            live = far & (jw >= start)
            w = jnp.where(far, jnp.where(live, kap, 0.0), ee[:, j0:]).astype(BF)
            dkap = jnp.where(live, pw, 0.0).astype(BF)
            rn = r[:, j0:] + jnp.where(far, 0.0, pw)
            if j0:
                r = jnp.concatenate([r[:, :j0], rn], axis=1)
            else:
                r = rn
            ds = (ee * r).astype(BF)
            dqa[rows, :] = dot_nn(ds, kaug[0, wide, 0:128])
            dka[wide, :] += dot_tn(ds, qaug[rows, 128:256])
            dva[wide, :] += dot_tn(eb, hhi)
            dva[win, :] += dot_tn(w, ghi)
            df = dot_nn(dkap, phk[0, win, :])
            if n:
                df = df + jnp.where(start < j0, dot_nt(ghi, states[n]), 0.0)
            dpq[rows, :] = df
            dpk[win, :] += dot_tn(dkap, phq[0, rows, :])
        back = None
        for n in reversed(range(T // CHUNK)):
            r0 = n * CHUNK
            j0 = max(r0 - BACK, 0)
            m = r0 + CHUNK - BACK - j0
            if back is not None:
                keys = pl.ds(j0, m)
                nstart = start_of(r0 + CHUNK, e0, e1)
                jc = j0 + lax.broadcasted_iota(jnp.int32, (m, 1), 0)
                bb = back.astype(BF)
                dpk[keys, :] += jnp.where(jc >= nstart, dot_nt(vaug[0, keys, :], bb), 0.0)
                dva[keys, :] += jnp.where(jc >= nstart, dot_nn(phk[0, keys, :], bb), 0.0)
                back = jnp.where(nstart < j0, back, 0.0)
            if n:
                rows = pl.ds(r0, CHUNK)
                start = start_col(r0, CHUNK, e0, e1)
                pq = jnp.where(start < j0, phq[0, rows, :].astype(F32), 0.0).astype(BF)
                add = dot_tn(pq, gvec[rows, :])
                back = add if back is None else back + add
        window = jnp.zeros((1, 128), F32)
        dmq = jnp.zeros((128, 128), F32)
        dmk = jnp.zeros((128, 128), F32)
        ones2 = jnp.concatenate([ones, ones], axis=0)
        for r0 in range(0, T, CHUNK):
            rows = pl.ds(r0, CHUNK)
            f = fq[rows, :]
            prod = f * (dpq[rows, :] * c)
            window = window + jnp.sum(prod, axis=0, keepdims=True)
            hi, lo = split2(prod)
            dp = (prod - f * dot_nn(jnp.concatenate([hi, lo], axis=1), ones2)).astype(BF)
            dmq = dmq + dot_tn(qaug[rows, 128:256], dp)
            dq = dqa[rows, :] * 0.125 + dot_nn(dp, mqt_ref[hh])
            dq = dq * cos_ref[rows, :] - spin(dq) * sin_ref[rows, :]
            keep = low if isinstance(hh, int) and hh == 0 else (low == (hh == 0))
            dq_ref[rows, :] = jnp.where(keep, dq, dq_ref[rows, :].astype(F32)).astype(BF)
            f = fk[rows, :]
            prod = f * dpk[rows, :]
            hi, lo = split2(prod)
            dp = (prod - f * dot_nn(jnp.concatenate([hi, lo], axis=1), ones2)).astype(BF)
            dmk = dmk + dot_tn(kaug[0, rows, 0:128], dp)
            dk_ref[rows, :] += dka[rows, :] * LN2 + dot_nn(dp, mkt_ref[hh])
            dv_ref[rows, :] += dva[rows, :]
        dmq = (dmq - swap(dmq)) * (8.0 * LN2)
        dmk = dmk - swap(dmk)
        gq_ref[hh] = dmq[0:64, 0:64]
        gk_ref[hh] = dmk[0:64, 0:64]
        st_ref[hh, 0:1, :] = square
        st_ref[hh, 1:2, :] = window
        return 0

    lax.fori_loop(0, 2, head, 0)

    for r0 in range(0, T, CHUNK):
        rows = pl.ds(r0, CHUNK)
        dk = dk_ref[rows, :]
        dk_ref[rows, :] = dk * cos_ref[rows, :] - spin(dk) * sin_ref[rows, :]


def rotary_tables(position):
    freq = 500000.0 ** (-2.0 * jnp.arange(32, dtype=F32) / 64)
    angle = position.astype(F32)[:, None] * freq[None, :]
    cosine, sine = jnp.cos(angle), jnp.sin(angle)
    return jnp.concatenate([cosine] * 4, axis=1), jnp.concatenate([-sine, sine] * 2, axis=1)


def pack_maps(maps, scale, keys):
    both = jnp.concatenate([maps, -maps], axis=2) * scale
    hi = lax.reduce_precision(both, 8, 7)
    lo = both - hi
    parts = [hi, lo, hi] if keys else [hi, hi, lo]
    return jnp.concatenate([*parts, jnp.zeros_like(lo)], axis=1).astype(BF)


def flip_maps(maps):
    both = jnp.swapaxes(jnp.concatenate([maps, -maps], axis=2), 1, 2)
    return jnp.concatenate([both, both], axis=2).astype(BF)


def attention_fwd(ends, cees, q, k, v, cosine, sine, mq, mk):
    T, H = q.shape[0], q.shape[1] // HD
    rep = 4
    full = lambda shape: pl.BlockSpec(shape, lambda p: (0,) * len(shape))
    pair = pl.BlockSpec((T, 128), lambda p: (0, p))
    heads = lambda *shape: pl.BlockSpec((2, *shape), lambda p: (p, 0, 0))
    smem = pl.BlockSpec(memory_space=pltpu.SMEM)
    return pl.pallas_call(
        functools.partial(fwd_kernel, rep=rep),
        grid=(H // 2,),
        in_specs=[smem, smem, pair, full((T, 128)), full((T, 128)), full((T, 128)), full((T, 128)),
                  heads(256, 128), heads(256, 128)],
        out_specs=[pair, heads(T, 128)],
        out_shape=[jax.ShapeDtypeStruct((T, H * HD), BF), jax.ShapeDtypeStruct((H, T, 128), F32)],
        scratch_shapes=[pltpu.VMEM((2, T, 256), BF), pltpu.VMEM((2, T, 128), BF), pltpu.VMEM((2, T, 256), BF),
                        pltpu.VMEM((2, T, 128), BF), pltpu.VMEM((2, T, 128), BF)],
        compiler_params=pltpu.CompilerParams(vmem_limit_bytes=48 * 2**20),
        cost_estimate=pl.CostEstimate(flops=H * 8 * 2**30, bytes_accessed=16 * 2**20, transcendentals=0),
        name="mix_forward",
    )(ends, cees, q, k, v, cosine, sine, mq, mk)


def attention_bwd(pair, ends, cees, q, k, v, cosine, sine, mq, mk, mqt, mkt, nm, da):
    T = q.shape[0]
    kv = 2 * pair // 4
    full = lambda shape: pl.BlockSpec(shape, lambda p: (0,) * len(shape))
    cols = pl.BlockSpec((T, 128), lambda p: (0, pair))
    heads = lambda *shape: pl.BlockSpec((2, *shape), lambda p: (pair, 0, 0))
    smem = pl.BlockSpec(memory_space=pltpu.SMEM)
    wide = full((T, 128))
    f32buf = pltpu.VMEM((T, 128), F32)
    return pl.pallas_call(
        functools.partial(bwd_kernel, pair=pair, kv=kv),
        grid=(1,),
        in_specs=[smem, smem, cols, wide, wide, wide, wide, heads(256, 128), heads(256, 128),
                  heads(128, 128), heads(128, 128), heads(T, 128), cols],
        out_specs=[wide, wide, wide, full((2, 64, 64)), full((2, 64, 64)), full((2, 8, 128))],
        out_shape=[jax.ShapeDtypeStruct((T, 128), BF), jax.ShapeDtypeStruct((T, 128), F32),
                   jax.ShapeDtypeStruct((T, 128), F32), jax.ShapeDtypeStruct((2, 64, 64), F32),
                   jax.ShapeDtypeStruct((2, 64, 64), F32), jax.ShapeDtypeStruct((2, 8, 128), F32)],
        scratch_shapes=[pltpu.VMEM((1, T, 256), BF), pltpu.VMEM((1, T, 128), BF),
                        pltpu.VMEM((T, 256), BF), f32buf, f32buf,
                        pltpu.VMEM((1, T, 128), BF), pltpu.VMEM((1, T, 128), BF),
                        pltpu.VMEM((T // CHUNK, 128, 128), BF), pltpu.VMEM((T, 128), BF),
                        f32buf, f32buf, f32buf, f32buf, f32buf],
        compiler_params=pltpu.CompilerParams(vmem_limit_bytes=56 * 2**20),
        cost_estimate=pl.CostEstimate(flops=30 * 10**9, bytes_accessed=8 * 2**20, transcendentals=0),
        name="mix_backward",
    )(ends, cees, q, k, v, cosine, sine, mq, mk, mqt, mkt, nm, da)


TILE = 256


def gated_kernel(x_ref, c_ref, wg_ref, wu_ref, wd_ref, *rest):
    act_ref, dg_ref, du_ref = rest[-3:]

    step = min(768, x_ref.shape[0])

    def some(n, _):
        rows = pl.ds(pl.multiple_of(n * step, step), step)
        x = x_ref[rows, :]
        gate = dot_nn(x, wg_ref[...])
        up = dot_nn(x, wu_ref[...])
        da = dot_nt(c_ref[rows, :], wd_ref[...])
        s = 1.0 / (1.0 + jnp.exp(-gate))
        gs = gate * s
        act_ref[rows, :] = (gs * up).astype(BF)
        du_ref[rows, :] = (da * gs).astype(BF)
        dg_ref[rows, :] = (da * up * (s + gs * (1.0 - s))).astype(BF)
        return 0

    lax.fori_loop(0, x_ref.shape[0] // step, some, 0)


def gated(x, cot, wg, wu, wd, part, parts, rows, row_block, group_rows, act, dg, du):
    width = x.shape[1]
    hidden = wg.shape[1] // parts
    tiles = hidden // TILE
    first = part * tiles
    blocks = x.shape[0] // rows
    left = pl.BlockSpec((rows, width), lambda n, r: (r, 0))
    column = pl.BlockSpec((width, TILE), lambda n, r: (0, first + n))
    tile = pl.BlockSpec((rows, TILE), lambda n, r: (row_block + r, n))
    wide = pl.BlockSpec((rows, TILE), lambda n, r: (row_block + r, first + n))
    specs = [left, left, column, column, pl.BlockSpec((TILE, width), lambda n, r: (first + n, 0))]
    args = [x, cot, wg, wu, wd]
    aliases = {}
    for k, value in enumerate((act, dg, du)):
        if value is not None:
            aliases[len(args)] = k
            args.append(value)
            specs.append(pl.BlockSpec(memory_space=pl.ANY))
    return pl.pallas_call(
        gated_kernel,
        grid=(tiles, blocks),
        in_specs=specs,
        out_specs=[tile, wide, wide],
        out_shape=[
            jax.ShapeDtypeStruct((group_rows, hidden), BF),
            jax.ShapeDtypeStruct((group_rows, hidden * parts), BF),
            jax.ShapeDtypeStruct((group_rows, hidden * parts), BF),
        ],
        input_output_aliases=aliases,
        compiler_params=pltpu.CompilerParams(vmem_limit_bytes=48 * 2**20),
        cost_estimate=pl.CostEstimate(
            flops=6 * x.shape[0] * width * hidden,
            bytes_accessed=4 * x.shape[0] * width + 6 * width * hidden,
            transcendentals=0,
        ),
        name="gated",
    )(*args)


ASKER_COUNT = 32
norm_eps = 1e-05
factored_multiplier = 2.0


def plain_contract(left, right):
    return jnp.dot(left, right, preferred_element_type=jnp.float32)


def transposed_right_product(left, right):
    return dot_nt(left, right)


def flipped_first_contract(left, right):
    return dot_tn(left, right)


def after(value, *done):
    return lax.optimization_barrier((value, *done))[0]


class Swaps:
    def __init__(self, axis):
        self.axis = axis
        self.count = lax.axis_size(axis)
        self.bits = self.count.bit_length() - 1
        self.me = lax.axis_index(axis)
        self.last = None

    def bit(self, b):
        return self.me // (1 << b) % 2

    def swap(self, value, b):
        return lax.ppermute(value, self.axis, [(i, i ^ (1 << b)) for i in range(self.count)])

    def queued(self, value, b):
        if self.last is not None:
            value = after(value, self.last)
        self.last = self.swap(value, b)
        return self.last


def row_order(mp):
    far = [0]
    for b in reversed(range(1, mp.bits)):
        far = far + [r ^ (1 << b) for r in far]
    far = far[1:]
    return [0, 1] + far + [r ^ 1 for r in far]


def gather_far(value, mp):
    rows = value.shape[0]
    for b in reversed(range(1, mp.bits)):
        got = mp.swap(value, b)
        value = got if mp.bits == 2 else jnp.concatenate([value, got], axis=0)
    return value if mp.bits == 2 else value[rows:]


def with_partner(value, mp):
    return jnp.concatenate([value, mp.swap(value, 0)], axis=0)


def scatter_rows(near, far, mp):
    half = far.shape[0] // 2
    got = mp.swap(far[half:], 0)
    far = (far[:half].astype(F32) + got.astype(F32)).astype(BF)
    rows = near.shape[0] // 2
    order = row_order(mp)[2 : 2 + half // rows]
    blocks = {r: far[k * rows : (k + 1) * rows] for k, r in enumerate(order)}
    got = mp.swap(near[rows:], 0)
    blocks[0] = near[:rows].astype(F32) + got.astype(F32)
    for b in reversed(range(1, mp.bits)):
        sent = [r for r in sorted(blocks) if r >> b & 1]
        send = [blocks.pop(r) for r in sent]
        got = mp.swap(send[0] if len(send) == 1 else jnp.concatenate(send, axis=0).astype(BF), b)
        for k, r in enumerate(sent):
            to = r ^ (1 << b)
            blocks[to] = blocks[to].astype(F32) + got[k * rows : (k + 1) * rows].astype(F32)
            if to:
                blocks[to] = blocks[to].astype(BF)
    return blocks[0]


def to_order(value, mp):
    order = row_order(mp)
    inverse = jnp.asarray([order.index(r) for r in range(mp.count)], jnp.int32)
    rows = value.shape[0] // mp.count
    blocks = [
        lax.dynamic_slice_in_dim(
            value, lax.dynamic_index_in_dim(inverse, a ^ mp.me, keepdims=False) * rows, rows, 0
        )
        for a in range(mp.count)
    ]
    return jnp.concatenate(blocks, axis=0)


def from_order(value, mp):
    rows = value.shape[0] // mp.count
    return [lax.dynamic_slice_in_dim(value, (mp.me ^ r) * rows, rows, 0) for r in row_order(mp)]


def take_half(value, index):
    half = value.shape[0] // 2
    return lax.dynamic_slice_in_dim(value, index * half, half, 0)


def place_kernel(at_ref, mine_ref, got_ref, *rest):
    first = pl.program_id(0) < pl.num_programs(0) // 2
    rest[-1][...] = jnp.where(first, mine_ref[...].astype(F32), got_ref[...].astype(F32))


def place(mine, got, at, into, part, parts):
    count = at.shape[0]
    rows, cols = mine.shape[0] * 2 // count, mine.shape[1]
    half = count // 2
    specs = [
        pl.BlockSpec((rows, cols), lambda r, at: (jnp.minimum(r, half - 1), 0)),
        pl.BlockSpec((rows, cols), lambda r, at: (jnp.maximum(r - half, 0), 0)),
    ]
    args = [at + part * count, mine, got]
    if into is not None:
        specs.append(pl.BlockSpec(memory_space=pl.ANY))
        args.append(into)
    return pl.pallas_call(
        place_kernel,
        grid_spec=pltpu.PrefetchScalarGridSpec(
            num_scalar_prefetch=1,
            grid=(count,),
            in_specs=specs,
            out_specs=pl.BlockSpec((rows, cols), lambda r, at: (at[r], 0)),
        ),
        out_shape=jax.ShapeDtypeStruct((mine.shape[0] * 2 * parts, cols), F32),
        input_output_aliases={} if into is None else {3: 0},
        compiler_params=pltpu.CompilerParams(vmem_limit_bytes=24 * 2**20),
        cost_estimate=pl.CostEstimate(
            flops=0, bytes_accessed=mine.shape[0] * cols * 12, transcendentals=0
        ),
        name="place",
    )(*args)


class Sum:
    def __init__(self, lane, part, at=0, parts=1):
        self.lane, self.at, self.parts = lane, at, parts
        for b in range(lane.bits):
            if b:
                part = (self.keep.astype(F32) + self.got.astype(F32)).astype(BF)
            self.keep = take_half(part, lane.bit(b))
            self.got = lane.queued(take_half(part, 1 - lane.bit(b)), b)

    def scatter(self, after=None):
        got = self.got
        if after is not None:
            got = lax.optimization_barrier((got, *(after if isinstance(after, tuple) else (after,))))[0]
        part = (self.keep.astype(F32) + got.astype(F32)).astype(BF)
        self.seen = part
        self.part = lax.psum_scatter(part, "z", scatter_dimension=0, tiled=True)
        self.value = lax.all_gather(self.part, "z", axis=0, tiled=True)

    def gather(self):
        lane = self.lane
        for b in reversed(range(lane.bits)):
            self.got = lane.queued(self.value, b)
            if b:
                self.value = jnp.concatenate([self.value, self.got], axis=0)

    def finish(self, into):
        lane = self.lane
        sub = 4
        steps = jnp.arange(lane.count * sub, dtype=jnp.int32)
        at = steps % sub
        for k, b in enumerate(reversed(range(lane.bits))):
            at = at + ((steps // sub // (1 << k) % 2) ^ lane.bit(b)) * (sub << k)
        return place(self.value, self.got, at, into, self.at, self.parts)


def pad_rows(value, rows):
    return jnp.pad(value, ((0, rows - value.shape[0]), (0, 0)))


def round_up(value, unit):
    return -(-value // unit) * unit


def rms_scale(values):
    return lax.rsqrt(jnp.mean(values * values, axis=-1, keepdims=True) + norm_eps)


def norm_back(values, scale_in, gain_in, grad_normed):
    weighted = grad_normed * gain_in
    grad_values = scale_in * weighted - values * (scale_in * scale_in * scale_in) * jnp.mean(
        weighted * values, axis=-1, keepdims=True
    )
    grad_gain = jnp.sum(grad_normed * values * scale_in, axis=0)
    return (grad_values, grad_gain)


def local(
    layer_tokens,
    sequence_extents,
    loss_sensitivity,
    mixing_rms_gain,
    asker_dense_map,
    lookup_dense_map,
    content_dense_map,
    shrink_map_asker,
    grow_map_asker,
    shrink_map_lookup,
    grow_map_lookup,
    shrink_map_content,
    grow_map_content,
    asker_feature_maps,
    lookup_feature_maps,
    local_portion_logit,
    emitted_mixing_map,
    emitted_shrink_map,
    emitted_grow_map,
    feedforward_rms_gain,
    gating_dense_map,
    widen_dense_map,
    shrink_dense_map,
):
    rows_dev = layer_tokens.shape[0]
    width = layer_tokens.shape[1]
    mp, lane = Swaps("mp"), Swaps("x")
    unit = 16 * lane.count * lax.axis_size("z")
    group_rows = rows_dev * lax.axis_size("mp")
    tokens_all = group_rows * lax.axis_size("z") * lax.axis_size("x")
    heads_dev = asker_dense_map.shape[1] // HD
    key_heads = lookup_dense_map.shape[1] // HD
    rank_width = shrink_map_asker.shape[1]
    first_end = sequence_extents[0, 0]
    second_end = first_end + sequence_extents[0, 1]
    ends = jnp.stack([first_end, second_end])
    places = jnp.arange(group_rows, dtype=jnp.int32)
    position = places - start_of(places, first_end, second_end)
    cosine, sine = rotary_tables(position)
    residual_in = layer_tokens.astype(jnp.float32)
    scale_one = rms_scale(residual_in)
    normalized_input = (residual_in * scale_one * mixing_rms_gain).astype(jnp.bfloat16)
    q_cols, k_cols = heads_dev * HD, key_heads * HD
    near_rows = 2 * rows_dev
    normed_near = with_partner(normalized_input, mp)
    normed_far = gather_far(normalized_input, mp)
    dense_all = jnp.concatenate(
        [asker_dense_map, lookup_dense_map, content_dense_map], axis=1
    )
    a_all_wide = jnp.concatenate([shrink_map_asker, shrink_map_lookup, shrink_map_content], axis=1)
    grow_all = jnp.concatenate(
        [
            jnp.pad(grow_map_asker, ((0, 0), (0, 2 * k_cols))),
            jnp.pad(grow_map_lookup, ((0, 0), (q_cols, k_cols))),
            jnp.pad(grow_map_content, ((0, 0), (q_cols + k_cols, 0))),
        ],
        axis=0,
    )
    dense_all = (
        dense_all.astype(F32) + factored_multiplier * plain_contract(a_all_wide, grow_all)
    ).astype(BF)
    mixing_map = (
        emitted_mixing_map.astype(F32)
        + factored_multiplier * plain_contract(emitted_shrink_map, emitted_grow_map)
    ).astype(BF)
    cees = jnp.exp(-local_portion_logit)
    tables = (
        pack_maps(asker_feature_maps, 8.0, False),
        pack_maps(lookup_feature_maps, LOG2E, True),
    )
    flipped = (flip_maps(asker_feature_maps), flip_maps(lookup_feature_maps))
    projected_near = plain_contract(normed_near, dense_all).astype(BF)
    normed_far = after(
        normed_far, dense_all, mixing_map, cees, cosine, sine, *tables, *flipped, projected_near
    )
    loss_far = gather_far(after(loss_sensitivity, normed_far), mp)
    normed_far = with_partner(normed_far, mp)
    projected_far = plain_contract(normed_far, dense_all).astype(BF)
    projected = to_order(jnp.concatenate([projected_near, projected_far], axis=0), mp)
    spare = max(0, 128 - k_cols)
    key_proj = jnp.pad(projected[:, q_cols : q_cols + k_cols], ((0, 0), (0, spare)))
    value_proj = jnp.pad(projected[:, q_cols + k_cols :], ((0, 0), (0, spare)))
    attention_args = (
        ends, cees, projected[:, :q_cols], key_proj, value_proj, cosine, sine, *tables
    )
    mixing_outcome, mixed_kept = attention_fwd(*attention_args)
    mixing_outcome, loss_far = lax.optimization_barrier((mixing_outcome, loss_far))
    mixing_blocks = from_order(mixing_outcome, mp)
    mixing_far = jnp.concatenate(mixing_blocks[2:], axis=0)
    mixing_near = jnp.concatenate(mixing_blocks[:2], axis=0)
    branch_far = plain_contract(mixing_far, mixing_map).astype(BF)
    branch_near = plain_contract(after(mixing_near, branch_far), mixing_map).astype(BF)
    hidden = residual_in + scatter_rows(branch_near, branch_far, mp)
    cot_later = after(loss_sensitivity, branch_near)
    cot_near = with_partner(cot_later, mp)
    cot_far = with_partner(loss_far, mp)
    cot_rows = jnp.concatenate([cot_near, cot_far], axis=0)
    hidden = after(hidden, cot_rows)
    scale_two = rms_scale(hidden)
    normed_two = (hidden * scale_two * feedforward_rms_gain).astype(BF)
    gathered_near = with_partner(normed_two, mp)
    gathered_far = gather_far(normed_two, mp)
    halves = 2
    acts = [None, None]
    d_gate = d_up = None
    for n in range(halves):
        acts[n], d_gate, d_up = gated(
            gathered_near, cot_near, gating_dense_map, widen_dense_map, shrink_dense_map,
            n, halves, near_rows, 0, group_rows, None, d_gate, d_up,
        )
    gathered_far = with_partner(after(gathered_far, d_gate), mp)
    downs = []
    for n in range(halves):
        acts[n], d_gate, d_up = gated(
            gathered_far, cot_far, gating_dense_map, widen_dense_map, shrink_dense_map,
            n, halves, near_rows, 1, group_rows, acts[n], d_gate, d_up,
        )
        downs.append(flipped_first_contract(acts[n], cot_rows).astype(BF))
        if n == 0:
            gathered_far = after(gathered_far, downs[0])
    down_one = Sum(lane, downs[0], parts=2)
    gathered_two = jnp.concatenate([gathered_near, gathered_far], axis=0)
    down_one.scatter(after=(downs[1], gathered_two))
    down_two = Sum(lane, downs[1], at=1, parts=2)
    gate_part = flipped_first_contract(after(gathered_two, down_one.seen), d_gate).astype(BF)
    through_gate = transposed_right_product(after(d_gate, gate_part), gating_dense_map)
    down_two.scatter(after=through_gate)
    gate_sum = Sum(lane, gate_part)
    d_normed_part = (
        through_gate + transposed_right_product(after(d_up, down_two.seen), widen_dense_map)
    ).astype(BF)
    collected_rows = jnp.concatenate([normed_near, normed_far], axis=0)
    mixing_outcome = jnp.concatenate([mixing_near, mixing_far], axis=0)
    middle_rows = plain_contract(after(collected_rows, d_normed_part), a_all_wide).astype(BF)
    emitted_inner_tokens = plain_contract(
        after(mixing_outcome, d_normed_part), emitted_shrink_map
    ).astype(BF)
    d_normed_two = scatter_rows(d_normed_part[:near_rows], d_normed_part[near_rows:], mp)
    up_part = flipped_first_contract(
        after(gathered_two, down_two.seen, down_one.value), d_up
    ).astype(BF)
    d_normed_two = after(d_normed_two, up_part)
    d_hidden_norm, grad_norm_two = norm_back(hidden, scale_two, feedforward_rms_gain, d_normed_two)
    d_hidden = loss_sensitivity.astype(F32) + d_hidden_norm
    d_branch = d_hidden.astype(BF)
    d_branch_near = with_partner(d_branch, mp)
    d_branch_far = gather_far(d_branch, mp)
    gate_sum.scatter(after=d_branch_near)
    d_branch_far = with_partner(after(d_branch_far, gate_sum.seen), mp)
    factored_path_derivative = jnp.concatenate([d_branch_near, d_branch_far], axis=0)
    d_attended = to_order(transposed_right_product(factored_path_derivative, mixing_map), mp)
    up_sum = Sum(lane, up_part)
    pairs = heads_dev // 2
    pair_outs = []
    for n in range(pairs):
        pair_outs.append(attention_bwd(n, *attention_args, *flipped, mixed_kept, d_attended))
        done = pair_outs[-1][0]
        d_attended = after(d_attended, done)
        if n == 0:
            d_attended = after(d_attended, down_two.value)
        if n == (pairs - 1) // 2:
            up_sum.scatter(after=d_attended)
            d_attended = after(d_attended, up_sum.seen)
            down_one.gather()
            down_two.gather()
        if n == pairs - 2:
            d_attended = after(d_attended, down_one.got)
    emitted_inner_derivative = (
        factored_multiplier * transposed_right_product(factored_path_derivative, emitted_grow_map)
    ).astype(BF)
    per_kv = pairs // key_heads
    d_keys, d_values = (
        jnp.concatenate(
            [
                sum(pair_outs[kv * per_kv + n][which][:, :HD] for n in range(per_kv))
                for kv in range(key_heads)
            ],
            axis=1,
        ).astype(BF)
        for which in (1, 2)
    )
    projected_gradient = jnp.concatenate(
        from_order(
            jnp.concatenate([outs[0] for outs in pair_outs] + [d_keys, d_values], axis=1), mp
        ),
        axis=0,
    )
    grad_query_maps = jnp.concatenate([outs[3] for outs in pair_outs], axis=0)
    grad_key_maps = jnp.concatenate([outs[4] for outs in pair_outs], axis=0)
    kept_sums = jnp.concatenate([outs[5] for outs in pair_outs], axis=0)
    combined_middle_gradient = (
        factored_multiplier * transposed_right_product(projected_gradient, grow_all)
    ).astype(BF)
    d_normed_part = transposed_right_product(projected_gradient, dense_all).astype(BF)
    d_normed = scatter_rows(d_normed_part[:near_rows], d_normed_part[near_rows:], mp)
    left = after(projected_gradient, d_normed_part, down_two.got)
    grad_w_all = flipped_first_contract(collected_rows, left)
    grow = factored_multiplier * flipped_first_contract(middle_rows, left)
    both = jnp.concatenate([grad_w_all.astype(BF), grow.astype(BF)], axis=0)
    proj_sum = Sum(lane, pad_rows(both, round_up(both.shape[0], unit)))
    half = shrink_dense_map.shape[0] // 2
    mlp_part = (
        plain_contract(after(acts[0], left), shrink_dense_map[:half])
        + plain_contract(acts[1], shrink_dense_map[half:])
    ).astype(BF)
    grad_w_down = down_two.finish(down_one.finish(None))
    gate_sum.gather()
    proj_sum.scatter()
    mlp_part = after(mlp_part, d_normed, gate_sum.got, grad_w_down, proj_sum.seen)
    output = (hidden + scatter_rows(mlp_part[:near_rows], mlp_part[near_rows:], mp)).astype(BF)
    grad_w_out = flipped_first_contract(mixing_outcome, factored_path_derivative).astype(BF)
    d_inputs_norm, grad_norm_one = norm_back(residual_in, scale_one, mixing_rms_gain, d_normed)
    input_grad = (d_hidden + d_inputs_norm).astype(BF)
    grad_a_all = flipped_first_contract(collected_rows, combined_middle_gradient)
    grad_a_out = flipped_first_contract(mixing_outcome, emitted_inner_derivative)
    emitted_grow_derivative = factored_multiplier * flipped_first_contract(
        emitted_inner_tokens, factored_path_derivative
    )
    shared = jnp.concatenate(
        [
            grad_norm_one[None],
            grad_norm_two[None],
            grad_a_all.T,
            emitted_grow_derivative,
            jnp.pad(jnp.sum(kept_sums[:, 0, :HD], axis=0), (0, width - HD))[None],
        ],
        axis=0,
    )

    for b in range(mp.bits):
        shared = shared + mp.swap(shared, b)
    n_shared = shared.shape[0]
    window_lanes = -kept_sums[:, 1, :]
    own = [grad_a_out, grad_query_maps, grad_key_maps, window_lanes]
    flat = jnp.concatenate([value.reshape(-1) for value in own])
    flat = jnp.pad(flat, (0, round_up(flat.shape[0], width) - flat.shape[0])).reshape(-1, width)
    last = jnp.concatenate([grad_w_out, shared.astype(BF), flat.astype(BF)], axis=0)
    out_sum = Sum(lane, pad_rows(last, round_up(last.shape[0], unit)))
    out_sum.scatter()
    up_sum.gather()
    grad_w_gate = gate_sum.finish(None)
    proj_sum.value = after(proj_sum.value, grad_w_gate)
    proj_sum.gather()
    grad_w_up = up_sum.finish(None)
    out_sum.value = after(out_sum.value, grad_w_up)
    out_sum.gather()
    total, last_total = proj_sum.finish(None), out_sum.finish(None)
    grad_w_query = total[:width, :q_cols]
    grad_w_key = total[:width, q_cols : q_cols + k_cols]
    grad_w_value = total[:width, q_cols + k_cols :]
    grow = total[width : width + 3 * rank_width]
    asker_grow_derivative = grow[:rank_width, :q_cols]
    lookup_grow_derivative = grow[rank_width : 2 * rank_width, q_cols : q_cols + k_cols]
    content_grow_derivative = grow[2 * rank_width : 3 * rank_width, q_cols + k_cols :]
    total = last_total
    out_rows = grad_w_out.shape[0]
    grad_w_out = total[:out_rows]
    shared = total[out_rows : out_rows + n_shared]
    grad_norm_one, grad_norm_two = shared[0], shared[1]
    grad_a_all = shared[2 : 2 + 3 * rank_width].T
    grad_a_query = grad_a_all[:, :rank_width]
    grad_a_key = grad_a_all[:, rank_width : 2 * rank_width]
    grad_a_value = grad_a_all[:, 2 * rank_width :]
    emitted_grow_derivative = shared[2 + 3 * rank_width : n_shared - 1]
    teacher_sq = jnp.sum(shared[n_shared - 1, :HD])
    flat = total[out_rows + n_shared :].reshape(-1)
    split = []
    for value in own:
        split.append(flat[: value.size].reshape(value.shape))
        flat = flat[value.size :]
    grad_a_out, grad_query_maps, grad_key_maps, window_lanes = split
    grad_window = jnp.sum(window_lanes, axis=1)
    teacher_mse = teacher_sq / float(tokens_all * ASKER_COUNT * HD)
    return (
        output,
        input_grad,
        grad_norm_one,
        grad_w_query,
        grad_w_key,
        grad_w_value,
        grad_a_query,
        asker_grow_derivative,
        grad_a_key,
        lookup_grow_derivative,
        grad_a_value,
        content_grow_derivative,
        grad_query_maps,
        grad_key_maps,
        grad_window,
        grad_w_out,
        grad_a_out,
        emitted_grow_derivative,
        grad_norm_two,
        grad_w_gate,
        grad_w_up,
        grad_w_down,
        teacher_mse,
    )


def solution(mesh):
    split = jax.sharding.Mesh(
        mesh.devices.reshape(4, mesh.shape["batch"] // 4, mesh.shape["mp"]), ("z", "x", "mp")
    )
    return jax.shard_map(
        local,
        mesh=split,
        in_specs=(
            P(("z", "x", "mp"), None),
            P(("z", "x"), None),
            P(("z", "x", "mp"), None),
            P(),
            P(None, "mp"),
            P(None, "mp"),
            P(None, "mp"),
            P(),
            P(None, "mp"),
            P(),
            P(None, "mp"),
            P(),
            P(None, "mp"),
            P("mp", None, None),
            P("mp", None, None),
            P("mp"),
            P("mp", None),
            P("mp", None),
            P(),
            P(),
            P(None, "mp"),
            P(None, "mp"),
            P("mp", None),
        ),
        out_specs=(
            P(("z", "x", "mp"), None),
            P(("z", "x", "mp"), None),
            P(),
            P(None, "mp"),
            P(None, "mp"),
            P(None, "mp"),
            P(),
            P(None, "mp"),
            P(),
            P(None, "mp"),
            P(),
            P(None, "mp"),
            P("mp", None, None),
            P("mp", None, None),
            P("mp"),
            P("mp", None),
            P("mp", None),
            P(),
            P(),
            P(None, "mp"),
            P(None, "mp"),
            P("mp", None),
            P(),
        ),
        check_vma=False,
    )
```

```python
import functools
import math
import jax
import jax.numpy as jnp
from jax import lax
from jax.experimental import pallas as pl
from jax.experimental.pallas import tpu as pltpu
from jax.sharding import PartitionSpec as P

HD = 64
WINDOW = 64
CHUNK = 256
BACK = 128
LOG2E = math.log2(math.e)
LN2 = math.log(2.0)
BIG = 16384.0
F32 = jnp.float32
BF = jnp.bfloat16


def dot_nn(a, b):
    return lax.dot_general(a, b, (((1,), (0,)), ((), ())), preferred_element_type=F32)


def dot_nt(a, b):
    return lax.dot_general(a, b, (((1,), (1,)), ((), ())), preferred_element_type=F32)


def dot_tn(a, b):
    return lax.dot_general(a, b, (((0,), (0,)), ((), ())), preferred_element_type=F32)


def lanes(rows):
    return lax.broadcasted_iota(jnp.int32, (rows, 128), 1)


def swap(x):
    return pltpu.roll(x, 64, 1)


def spin(x):
    lane = lanes(x.shape[0])
    return jnp.where((lane & 63) < 32, pltpu.roll(x, 96, 1), pltpu.roll(x, 32, 1))


def twin(x, odd):
    low = lanes(x.shape[0]) < 64
    other = swap(x)
    return jnp.where(low != odd, x, other)


def half_ones():
    r = lax.broadcasted_iota(jnp.int32, (128, 128), 0)
    c = lax.broadcasted_iota(jnp.int32, (128, 128), 1)
    return ((r < 64) == (c < 64)).astype(BF)


def start_of(t, e0, e1):
    return jnp.where(t >= e1, e1, jnp.where(t >= e0, e0, 0))


def start_col(r0, rows, e0, e1):
    t = r0 + lax.broadcasted_iota(jnp.int32, (rows, 1), 0)
    return start_of(t, e0, e1)


def prep_keys(k_ref, v_ref, cos_ref, sin_ref, kaug, vaug, seg, e0, e1, heads=(0, 1)):
    T = k_ref.shape[0]
    for r0 in range(0, T, CHUNK):
        rows = pl.ds(r0, CHUNK)
        k = k_ref[rows, :].astype(F32)
        v = v_ref[rows, :].astype(F32)
        kr = k * cos_ref[rows, :] + spin(k) * sin_ref[rows, :]
        lane = lanes(CHUNK)
        low = lane < 64
        if seg:
            t = r0 + lax.broadcasted_iota(jnp.int32, (CHUNK, 1), 0)
            mine = (t >= e0).astype(jnp.int32) + (t >= e1).astype(jnp.int32) + 64
            tail = jnp.where((lane < 67) & (lane != mine), -BIG, 0.0)
        else:
            tail = 0.0
        for at, kv in enumerate(heads):
            x = twin(kr, kv == 1)
            hi = x.astype(BF)
            lo = x - hi.astype(F32)
            kaug[at, rows, 0:128] = hi
            kaug[at, rows, 128:256] = jnp.where(low, lo, tail).astype(BF)
            vaug[at, rows, :] = jnp.where(low, v if kv == 0 else swap(v), 1.0).astype(BF)


def prep_query(qr, odd, seg, r0, e0, e1):
    x = twin(qr, odd)
    hi = x.astype(BF)
    lo = (x - hi.astype(F32)).astype(BF)
    lane = lanes(x.shape[0])
    low = lane < 64
    first = jnp.where(low, hi, lo)
    second = hi
    if seg:
        t = r0 + lax.broadcasted_iota(jnp.int32, (x.shape[0], 1), 0)
        mine = (t >= e0).astype(jnp.int32) + (t >= e1).astype(jnp.int32) + 64
        second = jnp.where(low, hi.astype(F32), jnp.where(lane == mine, 1.0, 0.0)).astype(BF)
    return first, second


def features(aug, maps, ones):
    p = jnp.exp2(dot_nn(aug, maps))
    return p / dot_nn(p.astype(BF), ones)


def fwd_kernel(e_ref, c_ref, q_ref, k_ref, v_ref, cos_ref, sin_ref, mq_ref, mk_ref,
               att_ref, nm_ref, kaug, vaug, qaug, phq, phk, *, rep):
    T = q_ref.shape[0]
    e0, e1 = e_ref[0], e_ref[1]
    p = pl.program_id(0)

    @pl.when(p == 0)
    def _():
        prep_keys(k_ref, v_ref, cos_ref, sin_ref, kaug, vaug, False, e0, e1)

    kv = (2 * p) // rep
    ones = half_ones()
    low = lanes(CHUNK) < 64
    for r0 in range(0, T, CHUNK):
        rows = pl.ds(r0, CHUNK)
        q = q_ref[rows, :].astype(F32) * (LOG2E / 8.0)
        qr = q * cos_ref[rows, :] + spin(q) * sin_ref[rows, :]
        for hh in range(2):
            first, second = prep_query(qr, hh == 1, False, r0, e0, e1)
            qaug[hh, rows, 0:128] = first
            qaug[hh, rows, 128:256] = second
            c = c_ref[2 * p + hh]
            phq[hh, rows, :] = (features(qaug[hh, rows, :], mq_ref[hh], ones) * c).astype(BF)
            phk[hh, rows, :] = features(kaug[kv, rows, :], mk_ref[hh], ones).astype(BF)
    for hh in range(2):
        state = None
        for r0 in range(0, T, CHUNK):
            rows = pl.ds(r0, CHUNK)
            j0 = max(r0 - BACK, 0)
            J = r0 + CHUNK - j0
            win = pl.ds(j0, J)
            ee = jnp.exp2(dot_nt(qaug[hh, rows, :], kaug[kv, win, :]))
            kap = dot_nt(phq[hh, rows, :], phk[hh, win, :])
            tt = r0 + lax.broadcasted_iota(jnp.int32, (CHUNK, J), 0)
            jj = j0 + lax.broadcasted_iota(jnp.int32, (CHUNK, J), 1)
            start = start_col(r0, CHUNK, e0, e1)
            w = jnp.where(tt - jj >= WINDOW, kap, ee)
            w = jnp.where((tt >= jj) & (jj >= start), w, 0.0)
            nd = dot_nn(w.astype(BF), vaug[kv, win, :])
            if state is not None:
                far = dot_nn(phq[hh, rows, :], state.astype(BF))
                nd = nd + jnp.where(start < j0, far, 0.0)
            rec = 1.0 / nd
            mix = nd * swap(rec)
            nm_ref[hh, rows, :] = jnp.where(low, mix, rec)
            if hh == 0:
                att_ref[rows, :] = mix.astype(BF)
            else:
                att_ref[rows, :] = jnp.where(low, att_ref[rows, :].astype(F32), swap(mix)).astype(BF)
            if r0 + CHUNK < T:
                state = next_state(state, phk, vaug, hh, kv, r0, j0, e0, e1)


def next_state(state, phk, vaug, hh, kv, r0, j0, e0, e1):
    n = r0 + CHUNK - BACK - j0
    nstart = start_of(r0 + CHUNK, e0, e1)
    jc = j0 + lax.broadcasted_iota(jnp.int32, (n, 1), 0)
    new = jnp.where(jc >= nstart, phk[hh, pl.ds(j0, n), :].astype(F32), 0.0).astype(BF)
    add = dot_tn(new, vaug[kv, pl.ds(j0, n), :])
    if state is None:
        return add
    return jnp.where(nstart < j0, state, 0.0) + add


def split2(x):
    hi = x.astype(BF)
    return hi, (x - hi.astype(F32)).astype(BF)


def bwd_kernel(e_ref, c_ref, q_ref, k_ref, v_ref, cos_ref, sin_ref, mq_ref, mk_ref, mqt_ref, mkt_ref,
               nm_ref, da_ref, dq_ref, dk_ref, dv_ref, gq_ref, gk_ref, st_ref,
               kaug, vaug, qaug, fq, fk, phq, phk, states, gvec, dpq, dpk, dqa, dva, dka, *, pair, kv):
    T = q_ref.shape[0]
    e0, e1 = e_ref[0], e_ref[1]
    prep_keys(k_ref, v_ref, cos_ref, sin_ref, kaug, vaug, True, e0, e1, (kv,))
    dk_ref[...] = jnp.zeros_like(dk_ref)
    dv_ref[...] = jnp.zeros_like(dv_ref)
    ones = half_ones()
    low = lanes(CHUNK) < 64
    lane = lanes(CHUNK)

    def head(hh, _):
        odd = hh == 1
        c = c_ref[2 * pair + hh]
        state = None
        for n, r0 in enumerate(range(0, T, CHUNK)):
            rows = pl.ds(r0, CHUNK)
            q = q_ref[rows, :].astype(F32) * (LOG2E / 8.0)
            qr = q * cos_ref[rows, :] + spin(q) * sin_ref[rows, :]
            first, second = prep_query(qr, odd, True, r0, e0, e1)
            qaug[rows, 0:128] = first
            qaug[rows, 128:256] = second
            f = features(qaug[rows, :], mq_ref[hh], ones)
            fq[rows, :] = f
            phq[0, rows, :] = (f * c).astype(BF)
            f = features(kaug[0, rows, :], mk_ref[hh], ones)
            fk[rows, :] = f
            phk[0, rows, :] = f.astype(BF)
            j0 = max(r0 - BACK, 0)
            if state is not None:
                states[n] = state.astype(BF)
            if r0 + CHUNK < T:
                state = next_state(state, phk, vaug, 0, 0, r0, j0, e0, e1)
        dpk[...] = jnp.zeros_like(dpk)
        dva[...] = jnp.zeros_like(dva)
        dka[...] = jnp.zeros_like(dka)
        square = jnp.zeros((1, 128), F32)
        for n, r0 in enumerate(range(0, T, CHUNK)):
            rows = pl.ds(r0, CHUNK)
            wide = pl.ds(0, r0 + CHUNK)
            diag = pl.ds(r0, CHUNK)
            tcol = r0 + lax.broadcasted_iota(jnp.int32, (CHUNK, 1), 0)
            start = start_of(tcol, e0, e1)
            full = r0 + CHUNK
            s = dot_nt(qaug[rows, :], kaug[0, wide, :])
            tt = r0 + lax.broadcasted_iota(jnp.int32, (CHUNK, full), 0)
            jj = lax.broadcasted_iota(jnp.int32, (CHUNK, full), 1)
            ee = jnp.exp2(s)
            ee = jnp.where(tt >= jj, ee, 0.0)
            eb = ee.astype(BF)
            nd = dot_nn(eb, vaug[0, wide, :])
            rec = 1.0 / nd
            soft = nd * swap(rec)
            soft = jnp.where(low, soft, swap(soft))
            srec = jnp.where(low, swap(rec), rec)
            nm = nm_ref[hh, rows, :]
            other = swap(nm)
            mix = jnp.where(low, nm, other)
            mrec = jnp.where(low, other, nm)
            delta = jnp.where(tcol < e1, mix - soft, 0.0)
            square = square + jnp.sum(delta * delta, axis=0, keepdims=True)
            g = twin(da_ref[rows, :], odd) + delta
            gd = -0.5 * jnp.sum(g * mix, axis=1, keepdims=True)
            gx = jnp.where(low, g, jnp.where(lane == 64, gd, 0.0)) * mrec
            hd = 0.5 * jnp.sum(delta * soft, axis=1, keepdims=True)
            hx = jnp.where(low, -delta, jnp.where(lane == 64, hd, 0.0)) * srec
            ghi, glo = split2(gx)
            hhi, hlo = split2(hx)
            gvec[rows, :] = ghi
            va = vaug[0, wide, :]
            r = dot_nt(jnp.concatenate([hhi, hlo], axis=1), jnp.concatenate([va, va], axis=1))
            j0 = max(r0 - BACK, 0)
            J = full - j0
            win = pl.ds(j0, J)
            vw = vaug[0, win, :]
            pw = dot_nt(jnp.concatenate([ghi, glo], axis=1), jnp.concatenate([vw, vw], axis=1))
            kap = dot_nt(phq[0, rows, :], phk[0, win, :])
            tw = r0 + lax.broadcasted_iota(jnp.int32, (CHUNK, J), 0)
            jw = j0 + lax.broadcasted_iota(jnp.int32, (CHUNK, J), 1)
            far = tw - jw >= WINDOW
            live = far & (jw >= start)
            w = jnp.where(far, jnp.where(live, kap, 0.0), ee[:, j0:]).astype(BF)
            dkap = jnp.where(live, pw, 0.0).astype(BF)
            rn = r[:, j0:] + jnp.where(far, 0.0, pw)
            if j0:
                r = jnp.concatenate([r[:, :j0], rn], axis=1)
            else:
                r = rn
            ds = (ee * r).astype(BF)
            dqa[rows, :] = dot_nn(ds, kaug[0, wide, 0:128])
            dka[wide, :] += dot_tn(ds, qaug[rows, 128:256])
            dva[wide, :] += dot_tn(eb, hhi)
            dva[win, :] += dot_tn(w, ghi)
            df = dot_nn(dkap, phk[0, win, :])
            if n:
                df = df + jnp.where(start < j0, dot_nt(ghi, states[n]), 0.0)
            dpq[rows, :] = df
            dpk[win, :] += dot_tn(dkap, phq[0, rows, :])
        back = None
        for n in reversed(range(T // CHUNK)):
            r0 = n * CHUNK
            j0 = max(r0 - BACK, 0)
            m = r0 + CHUNK - BACK - j0
            if back is not None:
                keys = pl.ds(j0, m)
                nstart = start_of(r0 + CHUNK, e0, e1)
                jc = j0 + lax.broadcasted_iota(jnp.int32, (m, 1), 0)
                bb = back.astype(BF)
                dpk[keys, :] += jnp.where(jc >= nstart, dot_nt(vaug[0, keys, :], bb), 0.0)
                dva[keys, :] += jnp.where(jc >= nstart, dot_nn(phk[0, keys, :], bb), 0.0)
                back = jnp.where(nstart < j0, back, 0.0)
            if n:
                rows = pl.ds(r0, CHUNK)
                start = start_col(r0, CHUNK, e0, e1)
                pq = jnp.where(start < j0, phq[0, rows, :].astype(F32), 0.0).astype(BF)
                add = dot_tn(pq, gvec[rows, :])
                back = add if back is None else back + add
        window = jnp.zeros((1, 128), F32)
        dmq = jnp.zeros((128, 128), F32)
        dmk = jnp.zeros((128, 128), F32)
        ones2 = jnp.concatenate([ones, ones], axis=0)
        for r0 in range(0, T, CHUNK):
            rows = pl.ds(r0, CHUNK)
            f = fq[rows, :]
            prod = f * (dpq[rows, :] * c)
            window = window + jnp.sum(prod, axis=0, keepdims=True)
            hi, lo = split2(prod)
            dp = (prod - f * dot_nn(jnp.concatenate([hi, lo], axis=1), ones2)).astype(BF)
            dmq = dmq + dot_tn(qaug[rows, 128:256], dp)
            dq = dqa[rows, :] * 0.125 + dot_nn(dp, mqt_ref[hh])
            dq = dq * cos_ref[rows, :] - spin(dq) * sin_ref[rows, :]
            keep = low if isinstance(hh, int) and hh == 0 else (low == (hh == 0))
            dq_ref[rows, :] = jnp.where(keep, dq, dq_ref[rows, :].astype(F32)).astype(BF)
            f = fk[rows, :]
            prod = f * dpk[rows, :]
            hi, lo = split2(prod)
            dp = (prod - f * dot_nn(jnp.concatenate([hi, lo], axis=1), ones2)).astype(BF)
            dmk = dmk + dot_tn(kaug[0, rows, 0:128], dp)
            dk_ref[rows, :] += dka[rows, :] * LN2 + dot_nn(dp, mkt_ref[hh])
            dv_ref[rows, :] += dva[rows, :]
        dmq = (dmq - swap(dmq)) * (8.0 * LN2)
        dmk = dmk - swap(dmk)
        gq_ref[hh] = dmq[0:64, 0:64]
        gk_ref[hh] = dmk[0:64, 0:64]
        st_ref[hh, 0:1, :] = square
        st_ref[hh, 1:2, :] = window
        return 0

    lax.fori_loop(0, 2, head, 0)

    for r0 in range(0, T, CHUNK):
        rows = pl.ds(r0, CHUNK)
        dk = dk_ref[rows, :]
        dk_ref[rows, :] = dk * cos_ref[rows, :] - spin(dk) * sin_ref[rows, :]


def rotary_tables(position):
    freq = 500000.0 ** (-2.0 * jnp.arange(32, dtype=F32) / 64)
    angle = position.astype(F32)[:, None] * freq[None, :]
    cosine, sine = jnp.cos(angle), jnp.sin(angle)
    return jnp.concatenate([cosine] * 4, axis=1), jnp.concatenate([-sine, sine] * 2, axis=1)


def pack_maps(maps, scale, keys):
    both = jnp.concatenate([maps, -maps], axis=2) * scale
    hi = lax.reduce_precision(both, 8, 7)
    lo = both - hi
    parts = [hi, lo, hi] if keys else [hi, hi, lo]
    return jnp.concatenate([*parts, jnp.zeros_like(lo)], axis=1).astype(BF)


def flip_maps(maps):
    both = jnp.swapaxes(jnp.concatenate([maps, -maps], axis=2), 1, 2)
    return jnp.concatenate([both, both], axis=2).astype(BF)


def attention_fwd(ends, cees, q, k, v, cosine, sine, mq, mk):
    T, H = q.shape[0], q.shape[1] // HD
    rep = 4
    full = lambda shape: pl.BlockSpec(shape, lambda p: (0,) * len(shape))
    pair = pl.BlockSpec((T, 128), lambda p: (0, p))
    heads = lambda *shape: pl.BlockSpec((2, *shape), lambda p: (p, 0, 0))
    smem = pl.BlockSpec(memory_space=pltpu.SMEM)
    return pl.pallas_call(
        functools.partial(fwd_kernel, rep=rep),
        grid=(H // 2,),
        in_specs=[smem, smem, pair, full((T, 128)), full((T, 128)), full((T, 128)), full((T, 128)),
                  heads(256, 128), heads(256, 128)],
        out_specs=[pair, heads(T, 128)],
        out_shape=[jax.ShapeDtypeStruct((T, H * HD), BF), jax.ShapeDtypeStruct((H, T, 128), F32)],
        scratch_shapes=[pltpu.VMEM((2, T, 256), BF), pltpu.VMEM((2, T, 128), BF), pltpu.VMEM((2, T, 256), BF),
                        pltpu.VMEM((2, T, 128), BF), pltpu.VMEM((2, T, 128), BF)],
        compiler_params=pltpu.CompilerParams(vmem_limit_bytes=48 * 2**20),
        cost_estimate=pl.CostEstimate(flops=H * 8 * 2**30, bytes_accessed=16 * 2**20, transcendentals=0),
        name="mix_forward",
    )(ends, cees, q, k, v, cosine, sine, mq, mk)


def attention_bwd(pair, ends, cees, q, k, v, cosine, sine, mq, mk, mqt, mkt, nm, da):
    T = q.shape[0]
    kv = 2 * pair // 4
    full = lambda shape: pl.BlockSpec(shape, lambda p: (0,) * len(shape))
    cols = pl.BlockSpec((T, 128), lambda p: (0, pair))
    heads = lambda *shape: pl.BlockSpec((2, *shape), lambda p: (pair, 0, 0))
    smem = pl.BlockSpec(memory_space=pltpu.SMEM)
    wide = full((T, 128))
    f32buf = pltpu.VMEM((T, 128), F32)
    return pl.pallas_call(
        functools.partial(bwd_kernel, pair=pair, kv=kv),
        grid=(1,),
        in_specs=[smem, smem, cols, wide, wide, wide, wide, heads(256, 128), heads(256, 128),
                  heads(128, 128), heads(128, 128), heads(T, 128), cols],
        out_specs=[wide, wide, wide, full((2, 64, 64)), full((2, 64, 64)), full((2, 8, 128))],
        out_shape=[jax.ShapeDtypeStruct((T, 128), BF), jax.ShapeDtypeStruct((T, 128), F32),
                   jax.ShapeDtypeStruct((T, 128), F32), jax.ShapeDtypeStruct((2, 64, 64), F32),
                   jax.ShapeDtypeStruct((2, 64, 64), F32), jax.ShapeDtypeStruct((2, 8, 128), F32)],
        scratch_shapes=[pltpu.VMEM((1, T, 256), BF), pltpu.VMEM((1, T, 128), BF),
                        pltpu.VMEM((T, 256), BF), f32buf, f32buf,
                        pltpu.VMEM((1, T, 128), BF), pltpu.VMEM((1, T, 128), BF),
                        pltpu.VMEM((T // CHUNK, 128, 128), BF), pltpu.VMEM((T, 128), BF),
                        f32buf, f32buf, f32buf, f32buf, f32buf],
        compiler_params=pltpu.CompilerParams(vmem_limit_bytes=56 * 2**20),
        cost_estimate=pl.CostEstimate(flops=30 * 10**9, bytes_accessed=8 * 2**20, transcendentals=0),
        name="mix_backward",
    )(ends, cees, q, k, v, cosine, sine, mq, mk, mqt, mkt, nm, da)


TILE = 256


def gated_kernel(x_ref, c_ref, wg_ref, wu_ref, wd_ref, *rest):
    act_ref, dg_ref, du_ref = rest[-3:]

    step = min(768, x_ref.shape[0])

    def some(n, _):
        rows = pl.ds(pl.multiple_of(n * step, step), step)
        x = x_ref[rows, :]
        gate = dot_nn(x, wg_ref[...])
        up = dot_nn(x, wu_ref[...])
        da = dot_nt(c_ref[rows, :], wd_ref[...])
        s = 1.0 / (1.0 + jnp.exp(-gate))
        gs = gate * s
        act_ref[rows, :] = (gs * up).astype(BF)
        du_ref[rows, :] = (da * gs).astype(BF)
        dg_ref[rows, :] = (da * up * (s + gs * (1.0 - s))).astype(BF)
        return 0

    lax.fori_loop(0, x_ref.shape[0] // step, some, 0)


def gated(x, cot, wg, wu, wd, part, parts, rows, row_block, group_rows, act, dg, du):
    width = x.shape[1]
    hidden = wg.shape[1] // parts
    tiles = hidden // TILE
    first = part * tiles
    blocks = x.shape[0] // rows
    left = pl.BlockSpec((rows, width), lambda n, r: (r, 0))
    column = pl.BlockSpec((width, TILE), lambda n, r: (0, first + n))
    tile = pl.BlockSpec((rows, TILE), lambda n, r: (row_block + r, n))
    wide = pl.BlockSpec((rows, TILE), lambda n, r: (row_block + r, first + n))
    specs = [left, left, column, column, pl.BlockSpec((TILE, width), lambda n, r: (first + n, 0))]
    args = [x, cot, wg, wu, wd]
    aliases = {}
    for k, value in enumerate((act, dg, du)):
        if value is not None:
            aliases[len(args)] = k
            args.append(value)
            specs.append(pl.BlockSpec(memory_space=pl.ANY))
    return pl.pallas_call(
        gated_kernel,
        grid=(tiles, blocks),
        in_specs=specs,
        out_specs=[tile, wide, wide],
        out_shape=[
            jax.ShapeDtypeStruct((group_rows, hidden), BF),
            jax.ShapeDtypeStruct((group_rows, hidden * parts), BF),
            jax.ShapeDtypeStruct((group_rows, hidden * parts), BF),
        ],
        input_output_aliases=aliases,
        compiler_params=pltpu.CompilerParams(vmem_limit_bytes=48 * 2**20),
        cost_estimate=pl.CostEstimate(
            flops=6 * x.shape[0] * width * hidden,
            bytes_accessed=4 * x.shape[0] * width + 6 * width * hidden,
            transcendentals=0,
        ),
        name="gated",
    )(*args)


ASKER_COUNT = 32
norm_eps = 1e-05
factored_multiplier = 2.0


def plain_contract(left, right):
    return jnp.dot(left, right, preferred_element_type=jnp.float32)


def transposed_right_product(left, right):
    return dot_nt(left, right)


def flipped_first_contract(left, right):
    return dot_tn(left, right)


def after(value, *done):
    return lax.optimization_barrier((value, *done))[0]


class Swaps:
    def __init__(self, axis):
        self.axis = axis
        self.count = lax.axis_size(axis)
        self.bits = self.count.bit_length() - 1
        self.me = lax.axis_index(axis)
        self.last = None

    def bit(self, b):
        return self.me // (1 << b) % 2

    def swap(self, value, b):
        return lax.ppermute(value, self.axis, [(i, i ^ (1 << b)) for i in range(self.count)])

    def queued(self, value, b):
        if self.last is not None:
            value = after(value, self.last)
        self.last = self.swap(value, b)
        return self.last


def row_order(mp):
    far = [0]
    for b in reversed(range(1, mp.bits)):
        far = far + [r ^ (1 << b) for r in far]
    far = far[1:]
    return [0, 1] + far + [r ^ 1 for r in far]


def gather_far(value, mp):
    rows = value.shape[0]
    for b in reversed(range(1, mp.bits)):
        got = mp.swap(value, b)
        value = got if mp.bits == 2 else jnp.concatenate([value, got], axis=0)
    return value if mp.bits == 2 else value[rows:]


def with_partner(value, mp):
    return jnp.concatenate([value, mp.swap(value, 0)], axis=0)


def scatter_rows(near, far, mp):
    half = far.shape[0] // 2
    got = mp.swap(far[half:], 0)
    far = (far[:half].astype(F32) + got.astype(F32)).astype(BF)
    rows = near.shape[0] // 2
    order = row_order(mp)[2 : 2 + half // rows]
    blocks = {r: far[k * rows : (k + 1) * rows] for k, r in enumerate(order)}
    got = mp.swap(near[rows:], 0)
    blocks[0] = near[:rows].astype(F32) + got.astype(F32)
    for b in reversed(range(1, mp.bits)):
        sent = [r for r in sorted(blocks) if r >> b & 1]
        send = [blocks.pop(r) for r in sent]
        got = mp.swap(send[0] if len(send) == 1 else jnp.concatenate(send, axis=0).astype(BF), b)
        for k, r in enumerate(sent):
            to = r ^ (1 << b)
            blocks[to] = blocks[to].astype(F32) + got[k * rows : (k + 1) * rows].astype(F32)
            if to:
                blocks[to] = blocks[to].astype(BF)
    return blocks[0]


def to_order(value, mp):
    order = row_order(mp)
    inverse = jnp.asarray([order.index(r) for r in range(mp.count)], jnp.int32)
    rows = value.shape[0] // mp.count
    blocks = [
        lax.dynamic_slice_in_dim(
            value, lax.dynamic_index_in_dim(inverse, a ^ mp.me, keepdims=False) * rows, rows, 0
        )
        for a in range(mp.count)
    ]
    return jnp.concatenate(blocks, axis=0)


def from_order(value, mp):
    rows = value.shape[0] // mp.count
    return [lax.dynamic_slice_in_dim(value, (mp.me ^ r) * rows, rows, 0) for r in row_order(mp)]


def take_half(value, index):
    half = value.shape[0] // 2
    return lax.dynamic_slice_in_dim(value, index * half, half, 0)


def place_kernel(at_ref, mine_ref, got_ref, *rest):
    first = pl.program_id(0) < pl.num_programs(0) // 2
    rest[-1][...] = jnp.where(first, mine_ref[...].astype(F32), got_ref[...].astype(F32))


def place(mine, got, at, into, part, parts):
    count = at.shape[0]
    rows, cols = mine.shape[0] * 2 // count, mine.shape[1]
    half = count // 2
    specs = [
        pl.BlockSpec((rows, cols), lambda r, at: (jnp.minimum(r, half - 1), 0)),
        pl.BlockSpec((rows, cols), lambda r, at: (jnp.maximum(r - half, 0), 0)),
    ]
    args = [at + part * count, mine, got]
    if into is not None:
        specs.append(pl.BlockSpec(memory_space=pl.ANY))
        args.append(into)
    return pl.pallas_call(
        place_kernel,
        grid_spec=pltpu.PrefetchScalarGridSpec(
            num_scalar_prefetch=1,
            grid=(count,),
            in_specs=specs,
            out_specs=pl.BlockSpec((rows, cols), lambda r, at: (at[r], 0)),
        ),
        out_shape=jax.ShapeDtypeStruct((mine.shape[0] * 2 * parts, cols), F32),
        input_output_aliases={} if into is None else {3: 0},
        compiler_params=pltpu.CompilerParams(vmem_limit_bytes=24 * 2**20),
        cost_estimate=pl.CostEstimate(
            flops=0, bytes_accessed=mine.shape[0] * cols * 12, transcendentals=0
        ),
        name="place",
    )(*args)


class Sum:
    def __init__(self, lane, part, at=0, parts=1):
        self.lane, self.at, self.parts = lane, at, parts
        for b in range(lane.bits):
            if b:
                part = (self.keep.astype(F32) + self.got.astype(F32)).astype(BF)
            self.keep = take_half(part, lane.bit(b))
            self.got = lane.queued(take_half(part, 1 - lane.bit(b)), b)

    def scatter(self, after=None, gather=True):
        got = self.got
        if after is not None:
            got = lax.optimization_barrier((got, *(after if isinstance(after, tuple) else (after,))))[0]
        part = (self.keep.astype(F32) + got.astype(F32)).astype(BF)
        self.seen = part
        self.part = lax.psum_scatter(part, "z", scatter_dimension=0, tiled=True)
        if gather:
            self.value = lax.all_gather(self.part, "z", axis=0, tiled=True)

    def gather(self):
        lane = self.lane
        for b in reversed(range(lane.bits)):
            self.got = lane.queued(self.value, b)
            if b:
                self.value = jnp.concatenate([self.value, self.got], axis=0)

    def finish(self, into):
        lane = self.lane
        sub = 4
        steps = jnp.arange(lane.count * sub, dtype=jnp.int32)
        at = steps % sub
        for k, b in enumerate(reversed(range(lane.bits))):
            at = at + ((steps // sub // (1 << k) % 2) ^ lane.bit(b)) * (sub << k)
        return place(self.value, self.got, at, into, self.at, self.parts)


def pad_rows(value, rows):
    return jnp.pad(value, ((0, rows - value.shape[0]), (0, 0)))


def round_up(value, unit):
    return -(-value // unit) * unit


def rms_scale(values):
    return lax.rsqrt(jnp.mean(values * values, axis=-1, keepdims=True) + norm_eps)


def norm_back(values, scale_in, gain_in, grad_normed):
    weighted = grad_normed * gain_in
    grad_values = scale_in * weighted - values * (scale_in * scale_in * scale_in) * jnp.mean(
        weighted * values, axis=-1, keepdims=True
    )
    grad_gain = jnp.sum(grad_normed * values * scale_in, axis=0)
    return (grad_values, grad_gain)


def local(
    layer_tokens,
    sequence_extents,
    loss_sensitivity,
    mixing_rms_gain,
    asker_dense_map,
    lookup_dense_map,
    content_dense_map,
    shrink_map_asker,
    grow_map_asker,
    shrink_map_lookup,
    grow_map_lookup,
    shrink_map_content,
    grow_map_content,
    asker_feature_maps,
    lookup_feature_maps,
    local_portion_logit,
    emitted_mixing_map,
    emitted_shrink_map,
    emitted_grow_map,
    feedforward_rms_gain,
    gating_dense_map,
    widen_dense_map,
    shrink_dense_map,
):
    rows_dev = layer_tokens.shape[0]
    width = layer_tokens.shape[1]
    mp, lane = Swaps("mp"), Swaps("x")
    unit = 16 * lane.count * lax.axis_size("z")
    group_rows = rows_dev * lax.axis_size("mp")
    tokens_all = group_rows * lax.axis_size("z") * lax.axis_size("x")
    heads_dev = asker_dense_map.shape[1] // HD
    key_heads = lookup_dense_map.shape[1] // HD
    rank_width = shrink_map_asker.shape[1]
    first_end = sequence_extents[0, 0]
    second_end = first_end + sequence_extents[0, 1]
    ends = jnp.stack([first_end, second_end])
    places = jnp.arange(group_rows, dtype=jnp.int32)
    position = places - start_of(places, first_end, second_end)
    cosine, sine = rotary_tables(position)
    residual_in = layer_tokens.astype(jnp.float32)
    scale_one = rms_scale(residual_in)
    normalized_input = (residual_in * scale_one * mixing_rms_gain).astype(jnp.bfloat16)
    q_cols, k_cols = heads_dev * HD, key_heads * HD
    near_rows = 2 * rows_dev
    normed_near = with_partner(normalized_input, mp)
    normed_far = gather_far(normalized_input, mp)
    dense_all = jnp.concatenate(
        [asker_dense_map, lookup_dense_map, content_dense_map], axis=1
    )
    a_all_wide = jnp.concatenate([shrink_map_asker, shrink_map_lookup, shrink_map_content], axis=1)
    grow_all = jnp.concatenate(
        [
            jnp.pad(grow_map_asker, ((0, 0), (0, 2 * k_cols))),
            jnp.pad(grow_map_lookup, ((0, 0), (q_cols, k_cols))),
            jnp.pad(grow_map_content, ((0, 0), (q_cols + k_cols, 0))),
        ],
        axis=0,
    )
    dense_all = (
        dense_all.astype(F32) + factored_multiplier * plain_contract(a_all_wide, grow_all)
    ).astype(BF)
    mixing_map = (
        emitted_mixing_map.astype(F32)
        + factored_multiplier * plain_contract(emitted_shrink_map, emitted_grow_map)
    ).astype(BF)
    cees = jnp.exp(-local_portion_logit)
    tables = (
        pack_maps(asker_feature_maps, 8.0, False),
        pack_maps(lookup_feature_maps, LOG2E, True),
    )
    flipped = (flip_maps(asker_feature_maps), flip_maps(lookup_feature_maps))
    projected_near = plain_contract(normed_near, dense_all).astype(BF)
    normed_far = after(
        normed_far, dense_all, mixing_map, cees, cosine, sine, *tables, *flipped, projected_near
    )
    loss_far = gather_far(after(loss_sensitivity, normed_far), mp)
    normed_far = with_partner(normed_far, mp)
    projected_far = plain_contract(normed_far, dense_all).astype(BF)
    projected = to_order(jnp.concatenate([projected_near, projected_far], axis=0), mp)
    spare = max(0, 128 - k_cols)
    key_proj = jnp.pad(projected[:, q_cols : q_cols + k_cols], ((0, 0), (0, spare)))
    value_proj = jnp.pad(projected[:, q_cols + k_cols :], ((0, 0), (0, spare)))
    attention_args = (
        ends, cees, projected[:, :q_cols], key_proj, value_proj, cosine, sine, *tables
    )
    mixing_outcome, mixed_kept = attention_fwd(*attention_args)
    mixing_outcome, loss_far = lax.optimization_barrier((mixing_outcome, loss_far))
    mixing_blocks = from_order(mixing_outcome, mp)
    mixing_far = jnp.concatenate(mixing_blocks[2:], axis=0)
    mixing_near = jnp.concatenate(mixing_blocks[:2], axis=0)
    branch_far = plain_contract(mixing_far, mixing_map).astype(BF)
    branch_near = plain_contract(after(mixing_near, branch_far), mixing_map).astype(BF)
    hidden = residual_in + scatter_rows(branch_near, branch_far, mp)
    cot_later = after(loss_sensitivity, branch_near)
    cot_near = with_partner(cot_later, mp)
    cot_far = with_partner(loss_far, mp)
    cot_rows = jnp.concatenate([cot_near, cot_far], axis=0)
    hidden = after(hidden, cot_rows)
    scale_two = rms_scale(hidden)
    normed_two = (hidden * scale_two * feedforward_rms_gain).astype(BF)
    gathered_near = with_partner(normed_two, mp)
    gathered_far = gather_far(normed_two, mp)
    halves = 2
    acts = [None, None]
    d_gate = d_up = None
    for n in range(halves):
        acts[n], d_gate, d_up = gated(
            gathered_near, cot_near, gating_dense_map, widen_dense_map, shrink_dense_map,
            n, halves, near_rows, 0, group_rows, None, d_gate, d_up,
        )
    gathered_far = with_partner(after(gathered_far, d_gate), mp)
    downs = []
    for n in range(halves):
        acts[n], d_gate, d_up = gated(
            gathered_far, cot_far, gating_dense_map, widen_dense_map, shrink_dense_map,
            n, halves, near_rows, 1, group_rows, acts[n], d_gate, d_up,
        )
        downs.append(flipped_first_contract(acts[n], cot_rows).astype(BF))
        if n == 0:
            gathered_far = after(gathered_far, downs[0])
    down_one = Sum(lane, downs[0], parts=2)
    gathered_two = jnp.concatenate([gathered_near, gathered_far], axis=0)
    down_one.scatter(after=(downs[1], gathered_two))
    down_two = Sum(lane, downs[1], at=1, parts=2)
    gate_part = flipped_first_contract(after(gathered_two, down_one.seen), d_gate).astype(BF)
    through_gate = transposed_right_product(after(d_gate, gate_part), gating_dense_map)
    down_two.scatter(after=through_gate)
    gate_sum = Sum(lane, gate_part)
    d_normed_part = (
        through_gate + transposed_right_product(after(d_up, down_two.seen), widen_dense_map)
    ).astype(BF)
    collected_rows = jnp.concatenate([normed_near, normed_far], axis=0)
    mixing_outcome = jnp.concatenate([mixing_near, mixing_far], axis=0)
    middle_rows = plain_contract(after(collected_rows, d_normed_part), a_all_wide).astype(BF)
    emitted_inner_tokens = plain_contract(
        after(mixing_outcome, d_normed_part), emitted_shrink_map
    ).astype(BF)
    d_normed_two = scatter_rows(d_normed_part[:near_rows], d_normed_part[near_rows:], mp)
    up_part = flipped_first_contract(
        after(gathered_two, down_two.seen, down_one.value), d_up
    ).astype(BF)
    d_normed_two = after(d_normed_two, up_part)
    d_hidden_norm, grad_norm_two = norm_back(hidden, scale_two, feedforward_rms_gain, d_normed_two)
    d_hidden = loss_sensitivity.astype(F32) + d_hidden_norm
    d_branch = d_hidden.astype(BF)
    d_branch_near = with_partner(d_branch, mp)
    d_branch_far = gather_far(d_branch, mp)
    gate_sum.scatter(after=d_branch_near)
    d_branch_far = with_partner(after(d_branch_far, gate_sum.seen), mp)
    factored_path_derivative = jnp.concatenate([d_branch_near, d_branch_far], axis=0)
    d_attended = to_order(transposed_right_product(factored_path_derivative, mixing_map), mp)
    up_sum = Sum(lane, up_part)
    pairs = heads_dev // 2
    pair_outs = []
    for n in range(pairs):
        pair_outs.append(attention_bwd(n, *attention_args, *flipped, mixed_kept, d_attended))
        done = pair_outs[-1][0]
        d_attended = after(d_attended, done)
        if n == 0:
            d_attended = after(d_attended, down_two.value)
        if n == (pairs - 1) // 2:
            up_sum.scatter(after=d_attended)
            d_attended = after(d_attended, up_sum.seen)
            down_one.gather()
            down_two.gather()
        if n == pairs - 2:
            d_attended = after(d_attended, down_one.got)
    emitted_inner_derivative = (
        factored_multiplier * transposed_right_product(factored_path_derivative, emitted_grow_map)
    ).astype(BF)
    per_kv = pairs // key_heads
    d_keys, d_values = (
        jnp.concatenate(
            [
                sum(pair_outs[kv * per_kv + n][which][:, :HD] for n in range(per_kv))
                for kv in range(key_heads)
            ],
            axis=1,
        ).astype(BF)
        for which in (1, 2)
    )
    projected_gradient = jnp.concatenate(
        from_order(
            jnp.concatenate([outs[0] for outs in pair_outs] + [d_keys, d_values], axis=1), mp
        ),
        axis=0,
    )
    grad_query_maps = jnp.concatenate([outs[3] for outs in pair_outs], axis=0)
    grad_key_maps = jnp.concatenate([outs[4] for outs in pair_outs], axis=0)
    kept_sums = jnp.concatenate([outs[5] for outs in pair_outs], axis=0)
    combined_middle_gradient = (
        factored_multiplier * transposed_right_product(projected_gradient, grow_all)
    ).astype(BF)
    d_normed_part = transposed_right_product(projected_gradient, dense_all).astype(BF)
    d_normed = scatter_rows(d_normed_part[:near_rows], d_normed_part[near_rows:], mp)
    left = after(projected_gradient, d_normed_part, down_two.got)
    grad_w_all = flipped_first_contract(collected_rows, left)
    d_normed = after(d_normed, grad_w_all)
    grow = factored_multiplier * flipped_first_contract(middle_rows, left)
    both = jnp.concatenate([grad_w_all.astype(BF), grow.astype(BF)], axis=0)
    proj_sum = Sum(lane, pad_rows(both, round_up(both.shape[0], unit)))
    half = shrink_dense_map.shape[0] // 2
    mlp_part = (
        plain_contract(after(acts[0], left), shrink_dense_map[:half])
        + plain_contract(acts[1], shrink_dense_map[half:])
    ).astype(BF)
    grad_w_down = down_two.finish(down_one.finish(None))
    gate_sum.gather()
    proj_sum.scatter(gather=False)
    mlp_part = after(mlp_part, d_normed, gate_sum.got, grad_w_down, proj_sum.seen)
    output = (hidden + scatter_rows(mlp_part[:near_rows], mlp_part[near_rows:], mp)).astype(BF)
    grad_w_out = flipped_first_contract(mixing_outcome, factored_path_derivative).astype(BF)
    d_inputs_norm, grad_norm_one = norm_back(residual_in, scale_one, mixing_rms_gain, d_normed)
    input_grad = (d_hidden + d_inputs_norm).astype(BF)
    grad_a_all = flipped_first_contract(collected_rows, combined_middle_gradient)
    grad_a_out = flipped_first_contract(mixing_outcome, emitted_inner_derivative)
    emitted_grow_derivative = factored_multiplier * flipped_first_contract(
        emitted_inner_tokens, factored_path_derivative
    )
    shared = jnp.concatenate(
        [
            grad_norm_one[None],
            grad_norm_two[None],
            grad_a_all.T,
            emitted_grow_derivative,
            jnp.pad(jnp.sum(kept_sums[:, 0, :HD], axis=0), (0, width - HD))[None],
        ],
        axis=0,
    )

    for b in range(mp.bits):
        shared = shared + mp.swap(shared, b)
    n_shared = shared.shape[0]
    window_lanes = -kept_sums[:, 1, :]
    own = [grad_a_out, grad_query_maps, grad_key_maps, window_lanes]
    flat = jnp.concatenate([value.reshape(-1) for value in own])
    flat = jnp.pad(flat, (0, round_up(flat.shape[0], width) - flat.shape[0])).reshape(-1, width)
    last = jnp.concatenate([grad_w_out, shared.astype(BF), flat.astype(BF)], axis=0)
    late = lax.psum_scatter(
        after(pad_rows(last, round_up(last.shape[0], unit)), up_sum.value),
        "z", scatter_dimension=0, tiled=True,
    )
    proj_sum.value = lax.all_gather(after(proj_sum.part, late), "z", axis=0, tiled=True)
    for b in range(lane.bits):
        got = lane.swap(take_half(late, 1 - lane.bit(b)), b)
        late = (take_half(late, lane.bit(b)).astype(F32) + got.astype(F32)).astype(BF)
    for b in reversed(range(lane.bits)):
        got = lane.swap(late, b)
        first = lane.bit(b) == 0
        late = jnp.concatenate([jnp.where(first, late, got), jnp.where(first, got, late)], axis=0)
    last_total = lax.all_gather(late, "z", axis=0, tiled=True).astype(F32)
    up_sum.gather()
    grad_w_gate = gate_sum.finish(None)
    proj_sum.value = after(proj_sum.value, grad_w_gate)
    proj_sum.gather()
    grad_w_up = up_sum.finish(None)
    total = proj_sum.finish(None)
    grad_w_query = total[:width, :q_cols]
    grad_w_key = total[:width, q_cols : q_cols + k_cols]
    grad_w_value = total[:width, q_cols + k_cols :]
    grow = total[width : width + 3 * rank_width]
    asker_grow_derivative = grow[:rank_width, :q_cols]
    lookup_grow_derivative = grow[rank_width : 2 * rank_width, q_cols : q_cols + k_cols]
    content_grow_derivative = grow[2 * rank_width : 3 * rank_width, q_cols + k_cols :]
    total = last_total
    out_rows = grad_w_out.shape[0]
    grad_w_out = total[:out_rows]
    shared = total[out_rows : out_rows + n_shared]
    grad_norm_one, grad_norm_two = shared[0], shared[1]
    grad_a_all = shared[2 : 2 + 3 * rank_width].T
    grad_a_query = grad_a_all[:, :rank_width]
    grad_a_key = grad_a_all[:, rank_width : 2 * rank_width]
    grad_a_value = grad_a_all[:, 2 * rank_width :]
    emitted_grow_derivative = shared[2 + 3 * rank_width : n_shared - 1]
    teacher_sq = jnp.sum(shared[n_shared - 1, :HD])
    flat = total[out_rows + n_shared :].reshape(-1)
    split = []
    for value in own:
        split.append(flat[: value.size].reshape(value.shape))
        flat = flat[value.size :]
    grad_a_out, grad_query_maps, grad_key_maps, window_lanes = split
    grad_window = jnp.sum(window_lanes, axis=1)
    teacher_mse = teacher_sq / float(tokens_all * ASKER_COUNT * HD)
    return (
        output,
        input_grad,
        grad_norm_one,
        grad_w_query,
        grad_w_key,
        grad_w_value,
        grad_a_query,
        asker_grow_derivative,
        grad_a_key,
        lookup_grow_derivative,
        grad_a_value,
        content_grow_derivative,
        grad_query_maps,
        grad_key_maps,
        grad_window,
        grad_w_out,
        grad_a_out,
        emitted_grow_derivative,
        grad_norm_two,
        grad_w_gate,
        grad_w_up,
        grad_w_down,
        teacher_mse,
    )


def solution(mesh):
    split = jax.sharding.Mesh(
        mesh.devices.reshape(4, mesh.shape["batch"] // 4, mesh.shape["mp"]), ("z", "x", "mp")
    )
    return jax.shard_map(
        local,
        mesh=split,
        in_specs=(
            P(("z", "x", "mp"), None),
            P(("z", "x"), None),
            P(("z", "x", "mp"), None),
            P(),
            P(None, "mp"),
            P(None, "mp"),
            P(None, "mp"),
            P(),
            P(None, "mp"),
            P(),
            P(None, "mp"),
            P(),
            P(None, "mp"),
            P("mp", None, None),
            P("mp", None, None),
            P("mp"),
            P("mp", None),
            P("mp", None),
            P(),
            P(),
            P(None, "mp"),
            P(None, "mp"),
            P("mp", None),
        ),
        out_specs=(
            P(("z", "x", "mp"), None),
            P(("z", "x", "mp"), None),
            P(),
            P(None, "mp"),
            P(None, "mp"),
            P(None, "mp"),
            P(),
            P(None, "mp"),
            P(),
            P(None, "mp"),
            P(),
            P(None, "mp"),
            P("mp", None, None),
            P("mp", None, None),
            P("mp"),
            P("mp", None),
            P("mp", None),
            P(),
            P(),
            P(None, "mp"),
            P(None, "mp"),
            P("mp", None),
            P(),
        ),
        check_vma=False,
    )
```
